32 devices in a mesh: wide: 8 (over y, x, core), narrow: 4 (over z).
Axes of the slice: x: 2, y: 2, z: 4, core: 2. Of those that a mesh axis runs over, the one named last changes fastest.
Arguments:
- initial: float32 [64, 64, 128, 128], P(None, 'wide', 'narrow'), may hold values from 0.2 to 1.8
- target: float32 [64, 64, 128, 128], P(None, 'wide', 'narrow'), may hold values from 0.2 to 1.8
- rates_small: float32 [2, 64, 64], replicated, may hold values from 0.1 to 1
- rates_large: float32 [2, 128, 128], replicated, may hold values from 0.1 to 1
- pattern_small: int32 [2, 64, 64], replicated, may hold values 0 or 1
- pattern_large: int32 [2, 128, 128], replicated, may hold values 0 or 1
- spare_small: float32 [64, 64], replicated, may hold values from 0.02 to 0.2
- spare_large: float32 [128, 128], replicated, may hold values from 0.02 to 0.2
- trigger_first: int32 [64], replicated, may hold values 0 or 1
- trigger_last: int32 [128], replicated, may hold values 0 or 1
Outputs:
- grad_small: float32 [2, 64, 64], replicated
- grad_large: float32 [2, 128, 128], replicated
The draws below stay inside these ranges and needn't reach their ends.
All inputs are finite; a program needn't handle non-finite values.
Results may differ from the reference program's by a relative error of at most 0.00005.
Values sent between devices are 32-bit elements; how exact they have to be, the bound alone decides.
No kernel may reach another device: no remote copies, remote signals or barrier semaphores. Data moves between devices by JAX's collectives and lax.ppermute only.
A program may use at most 192 MiB of HBM per device.

```python
import math
import jax
import jax.numpy as jnp
from jax import lax

SA = 64
SB = 128


def place_ends(array, own_key, least, top_value):
    index_at = [jax.random.randint(jax.random.fold_in(own_key, axis), (), 0, length) for axis, length in enumerate(array.shape)]
    longest = array.shape.index(max(array.shape))
    neighbour = index_at[:longest] + [(index_at[longest] + 1) % array.shape[longest]] + index_at[longest + 1:]
    return array.at[tuple(index_at)].set(least).at[tuple(neighbour)].set(top_value)


def shard_levels(own_key, dims, cuts, low, top_value):
    gain = 1.0
    for axis_at, parts in cuts:
        heights = jax.random.uniform(jax.random.fold_in(jax.random.fold_in(own_key, 6), axis_at), (parts,), jnp.float32, low / len(cuts), top_value / len(cuts))
        gain = gain * jnp.repeat(jnp.exp(heights), dims[axis_at] // parts).reshape((-1,) + (1,) * (len(dims) - 1 - axis_at))
    return gain


def setup_inputs(seed: int = 0) -> dict:
    arg_keys = jax.random.split(jax.random.key(seed), 11)
    initial = jnp.clip(0.2 + 1.5999999 * jax.random.uniform(arg_keys[0], (SA, SA, SB, SB), jnp.float32) ** shard_levels(arg_keys[0], (SA, SA, SB, SB), ((1, 8), (2, 4)), -0.2, 0.2), 0.2, 1.8)
    target = jnp.clip(0.2 + 1.5999999 * jax.random.uniform(arg_keys[1], (SA, SA, SB, SB), jnp.float32) ** shard_levels(arg_keys[1], (SA, SA, SB, SB), ((1, 8), (2, 4)), -0.2, 0.2), 0.2, 1.8)
    rates_small = jnp.clip(jnp.exp(jax.random.uniform(arg_keys[2], (2, SA, SA), jnp.float32, math.log(0.1), math.log(1.0))), 0.1, 1.0)
    rates_large = jnp.clip(jnp.exp(jax.random.uniform(arg_keys[3], (2, SB, SB), jnp.float32, math.log(0.1), math.log(1.0))), 0.1, 1.0)
    pattern_small = place_ends((jax.random.randint(arg_keys[4], (2, SA, SA), 0, 4) < 1).astype(jnp.int32), jax.random.fold_in(arg_keys[4], 1), 0, 1)
    pattern_large = place_ends((jax.random.randint(arg_keys[5], (2, SB, SB), 0, 4) < 1).astype(jnp.int32), jax.random.fold_in(arg_keys[5], 1), 0, 1)
    spare_small = jnp.clip(jnp.exp(jax.random.uniform(arg_keys[6], (SA, SA), jnp.float32, math.log(0.02), math.log(0.2))), 0.02, 0.2)
    spare_large = jnp.clip(jnp.exp(jax.random.uniform(arg_keys[7], (SB, SB), jnp.float32, math.log(0.02), math.log(0.2))), 0.02, 0.2)
    trigger_first = place_ends((jax.random.randint(arg_keys[8], (SA,), 0, 2) < 1).astype(jnp.int32), jax.random.fold_in(arg_keys[8], 1), 0, 1)
    trigger_last = place_ends((jax.random.randint(arg_keys[9], (SB,), 0, 2) < 1).astype(jnp.int32), jax.random.fold_in(arg_keys[9], 1), 0, 1)
    return {"initial": initial, "target": target, "rates_small": rates_small, "rates_large": rates_large, "pattern_small": pattern_small, "pattern_large": pattern_large, "spare_small": spare_small, "spare_large": spare_large, "trigger_first": trigger_first, "trigger_last": trigger_last}


highest = lax.Precision.HIGHEST

def generator(rate_matrix, pattern):
    extent = rate_matrix.shape[-1]
    identity = jnp.eye(extent, dtype=jnp.float32)
    opened = pattern.astype(jnp.float32) * (1.0 - identity)
    flow_rates = rate_matrix * opened
    leaving = lax.optimization_barrier(jnp.sum(flow_rates, axis=-1))
    return (flow_rates - leaving[..., :, None] * identity, leaving, opened)

def operate(tensor, matrices, weight_first, weight_last):
    mode_zero, mode_one, mode_two, mode_three, spare_one, spare_two, rim_one, rim_two = matrices
    summed = jnp.einsum('abcd,ae->ebcd', tensor, mode_zero, precision=highest)
    summed = summed + jnp.einsum('abcd,be->aecd', tensor, mode_one, precision=highest)
    summed = summed + jnp.einsum('abcd,ce->abed', tensor, mode_two, precision=highest)
    summed = summed + jnp.einsum('abcd,de->abce', tensor, mode_three, precision=highest)
    lifted = tensor * weight_first[:, None, None, None]
    summed = summed + jnp.einsum('abcd,be->aecd', lifted, spare_one, precision=highest) - lifted * rim_one[None, :, None, None]
    lowered = tensor * weight_last[None, None, None, :]
    summed = summed + jnp.einsum('abcd,ce->abed', lowered, spare_two, precision=highest) - lowered * rim_two[None, None, :, None]
    return summed

def reference(initial, target, rates_small, rates_large, pattern_small, pattern_large, spare_small, spare_large, trigger_first, trigger_last):
    gen_small, exit_small, open_small = generator(rates_small, pattern_small)
    gen_large, exit_large, open_large = generator(rates_large, pattern_large)
    rim_one = lax.optimization_barrier(jnp.sum(spare_small, axis=1))
    rim_two = lax.optimization_barrier(jnp.sum(spare_large, axis=1))
    weight_first = trigger_first.astype(jnp.float32)
    weight_last = trigger_last.astype(jnp.float32)
    bound = jnp.sum(lax.optimization_barrier(jnp.max(exit_small, axis=1))) + jnp.sum(lax.optimization_barrier(jnp.max(exit_large, axis=1)))
    bound = bound + jnp.max(weight_first) * jnp.max(rim_one) + jnp.max(weight_last) * jnp.max(rim_two)
    step_size = 1.0 / bound
    onward = (gen_small[0], gen_small[1], gen_large[0], gen_large[1], spare_small, spare_large, rim_one, rim_two)
    state = initial + step_size * operate(initial, onward, weight_first, weight_last)
    adjoint = state - target
    cross_zero = jnp.einsum('abcd,ebcd->ae', initial, adjoint, precision=highest)
    cross_one = jnp.einsum('abcd,aecd->be', initial, adjoint, precision=highest)
    cross_two = jnp.einsum('abcd,abed->ce', initial, adjoint, precision=highest)
    cross_three = jnp.einsum('abcd,abce->de', initial, adjoint, precision=highest)
    small = jnp.stack([cross_zero, cross_one]) / math.sqrt(SA * SB * SB)
    large = jnp.stack([cross_two, cross_three]) / math.sqrt(SA * SA * SB)
    grad_small = open_small * (small - jnp.diagonal(small, axis1=1, axis2=2)[:, :, None])
    grad_large = open_large * (large - jnp.diagonal(large, axis1=1, axis2=2)[:, :, None])
    return (grad_small, grad_large)
```

```python
import functools
import math

import jax
import jax.numpy as jnp
from jax import lax
from jax.experimental import pallas as pl
from jax.experimental.pallas import tpu as pltpu
from jax.sharding import PartitionSpec as P

highest = lax.Precision.HIGHEST
f32 = jnp.float32
VMEM_LIMIT = 40 * 1024 * 1024
bf16 = jnp.bfloat16

TO_INNER = [(0, 1), (3, 2)]
INNER_SWAP = [(1, 2), (2, 1)]
TO_OUTER = [(1, 0), (2, 3)]

PIECES = [(0, 2), (2, 4), (4, 6), (6, 7), (7, 8)]

ROWS_BY_ROWS = (((1,), (1,)), ((), ()))
DEPTH_BY_DEPTH = (((0,), (0,)), ((), ()))


def generator(rate_matrix, pattern):
    extent = rate_matrix.shape[-1]
    identity = jnp.eye(extent, dtype=jnp.float32)
    opened = pattern.astype(jnp.float32) * (1.0 - identity)
    flow_rates = rate_matrix * opened
    leaving = jnp.sum(flow_rates, axis=-1)
    return (flow_rates - leaving[..., :, None] * identity, leaving, opened)


def halves(value):
    high = value.astype(bf16)
    low = (value - high.astype(f32)).astype(bf16)
    return high, low


def all_sum(value, axes):
    for axis in axes:
        extent = lax.axis_size(axis)
        step = 1
        while step < extent:
            pairs = [(i, i ^ step) for i in range(extent)]
            value = value + lax.ppermute(value, axis, pairs)
            step *= 2
    return value


def whole(array):
    return pl.BlockSpec(array.shape, lambda i: (0,) * array.ndim)


def stacked_rows(ref, count, inner, at):
    rows = [ref[pl.ds(at + k, count, stride=inner), :] for k in (0, 1)]
    high, low = halves(jnp.concatenate(rows, axis=1))
    return jnp.concatenate([high, low], axis=0)


def left_parts(matrix):
    high, low = halves(matrix)
    return jnp.concatenate(
        [jnp.concatenate([high, high], axis=1), jnp.concatenate([low, low], axis=1)], axis=0
    )


def folded(total):
    rows, cols = total.shape[0] // 2, total.shape[1] // 2
    total = total[:rows] + total[rows:]
    return total[:, :cols] + total[:, cols:]


def product(matrix, in_ref, out_ref, count, inner, add):
    width = in_ref.shape[1]
    for at in range(0, inner, 2):
        out = jnp.dot(matrix, stacked_rows(in_ref, count, inner, at), preferred_element_type=f32)
        out = out[:count] + out[count:]
        for k in (0, 1):
            place = pl.ds(at + k, count, stride=inner)
            piece = out[:, k * width : (k + 1) * width]
            out_ref[place, :] = out_ref[place, :] + piece if add else piece


def base_body(x_ref, t_ref, first_ref, last_ref, o_ref):
    count, _, inner, width = x_ref.shape
    x2, t2, o2 = (ref.reshape(count * inner, width) for ref in (x_ref, t_ref, o_ref))
    high, low = halves(last_ref[...])
    last = jnp.concatenate([jnp.concatenate([high, low], axis=1)] * 2, axis=0)
    for r in range(0, count * inner, 256):
        x = x2[r : r + 256]
        high, low = halves(x)
        out = jnp.dot(jnp.concatenate([high, low], axis=1), last, preferred_element_type=f32)
        o2[r : r + 256] = x - t2[r : r + 256] + (out[:, :width] + out[:, width:])
    product(left_parts(first_ref[...]), x2, o2, count, inner, True)


def base_terms(x, t, first, last):
    block = pl.BlockSpec((x.shape[0], 1) + x.shape[2:], lambda i: (0, i, 0, 0))
    return pl.pallas_call(
        base_body,
        grid=(x.shape[1],),
        in_specs=[block, block, whole(first), whole(last)],
        out_specs=block,
        out_shape=jax.ShapeDtypeStruct(x.shape, f32),
        compiler_params=pltpu.CompilerParams(vmem_limit_bytes=VMEM_LIMIT),
        cost_estimate=pl.CostEstimate(flops=x.size * 4096, bytes_accessed=x.size * 12, transcendentals=0),
    )(x, t, first, last)


def one_body(x_ref, k_ref, o_ref):
    blocks, _, rows, inner, width = x_ref.shape
    count = blocks * rows
    x2, o2 = x_ref.reshape(count * inner, width), o_ref.reshape(count * inner, width)
    product(left_parts(k_ref[0]), x2, o2, count, inner, False)


def one_terms(x, matrices):
    block = pl.BlockSpec((x.shape[0], 1) + x.shape[2:], lambda i: (0, i, 0, 0, 0))
    return pl.pallas_call(
        one_body,
        grid=(x.shape[1],),
        in_specs=[block, pl.BlockSpec((1,) + matrices.shape[1:], lambda i: (i, 0, 0))],
        out_specs=block,
        out_shape=jax.ShapeDtypeStruct(x.shape, f32),
        compiler_params=pltpu.CompilerParams(vmem_limit_bytes=VMEM_LIMIT),
        cost_estimate=pl.CostEstimate(flops=x.size * 4096, bytes_accessed=x.size * 8, transcendentals=0),
    )(x, matrices)


def one_cross_body(x_ref, a_ref, o_ref):
    blocks, _, rows, inner, width = x_ref.shape
    count = blocks * rows
    x2, a2 = x_ref.reshape(count * inner, width), a_ref.reshape(count * inner, width)
    total = None
    for at in range(0, inner, 2):
        term = lax.dot_general(
            stacked_rows(x2, count, inner, at),
            stacked_rows(a2, count, inner, at),
            ROWS_BY_ROWS,
            preferred_element_type=f32,
        )
        total = term if total is None else total + term
    o_ref[0] = folded(total)


def one_cross(x, a, skip):
    count = x.shape[0] * x.shape[2]
    shape = (x.shape[0], 1) + x.shape[2:]
    out = pl.pallas_call(
        one_cross_body,
        grid=(a.shape[1],),
        in_specs=[
            pl.BlockSpec(shape, lambda i: (0, i + skip, 0, 0, 0)),
            pl.BlockSpec(shape, lambda i: (0, i, 0, 0, 0)),
        ],
        out_specs=pl.BlockSpec((1, count, count), lambda i: (i, 0, 0)),
        out_shape=jax.ShapeDtypeStruct((a.shape[1], count, count), f32),
        compiler_params=pltpu.CompilerParams(vmem_limit_bytes=VMEM_LIMIT),
        cost_estimate=pl.CostEstimate(flops=a.size * 4096, bytes_accessed=a.size * 8, transcendentals=0),
    )(x, a)
    return out


def local_body(pieces, x_ref, *refs):
    a_refs, o_ref, o3_ref = refs[: len(pieces)], refs[-2], refs[-1]
    wide, deep, _, inner, width = x_ref.shape
    x2 = x_ref.reshape(wide * deep * inner, width)
    flat = [a.reshape(a.shape[0] * a.shape[1] * inner, width) for a in a_refs]
    total = None
    for at in range(0, inner, 2):
        parts = []
        for k in (0, 1):
            rows = [
                a[pl.ds(at + k, wide * (hi - lo), stride=inner), :] for a, (lo, hi) in zip(flat, pieces)
            ]
            parts.append(jnp.concatenate(rows, axis=0))
        high, low = halves(jnp.concatenate(parts, axis=1))
        term = lax.dot_general(
            stacked_rows(x2, wide * deep, inner, at),
            jnp.concatenate([high, low], axis=0),
            ROWS_BY_ROWS,
            preferred_element_type=f32,
        )
        total = term if total is None else total + term
    o_ref[0] = folded(total)
    total = None
    for a_ref, (lo, hi) in zip(a_refs, pieces):
        for s in range(lo, hi):
            sides = []
            for ref, at in ((x_ref, s), (a_ref, s - lo)):
                rows = jnp.concatenate([ref[w, at, 0] for w in range(wide)], axis=0)
                sides.append(jnp.concatenate(halves(rows), axis=1))
            term = lax.dot_general(sides[0], sides[1], DEPTH_BY_DEPTH, preferred_element_type=f32)
            total = term if total is None else total + term
    o3_ref[0] = folded(total)


def local_cross(x, adjoints):
    wide, deep, rows, inner, width = x.shape
    block = lambda a: pl.BlockSpec((wide, a.shape[1], 1, inner, width), lambda i: (0, 0, i, 0, 0))
    count = wide * deep
    zero, three = pl.pallas_call(
        functools.partial(local_body, PIECES),
        grid=(rows,),
        in_specs=[block(x)] + [block(a) for a in adjoints],
        out_specs=[
            pl.BlockSpec((1, count, count), lambda i: (i, 0, 0)),
            pl.BlockSpec((1, width, width), lambda i: (i, 0, 0)),
        ],
        out_shape=[
            jax.ShapeDtypeStruct((rows, count, count), f32),
            jax.ShapeDtypeStruct((rows, width, width), f32),
        ],
        compiler_params=pltpu.CompilerParams(vmem_limit_bytes=VMEM_LIMIT),
        cost_estimate=pl.CostEstimate(flops=x.size * 4096, bytes_accessed=x.size * 8, transcendentals=0),
    )(x, *adjoints)
    zero = jnp.sum(zero, axis=0)
    columns, at = [], 0
    for lo, hi in PIECES:
        size = wide * (hi - lo)
        columns.append(zero[:, at : at + size].reshape(count, wide, hi - lo))
        at += size
    zero = jnp.concatenate(columns, axis=2).reshape(count, count)
    return zero, jnp.sum(three, axis=0)


def inner_body(slabs, w_ref, m_ref, x_ref, p_ref, q_ref, f_ref, b_ref, bp_ref, a_ref, y_ref, c_ref):
    part = x_ref.shape[1]
    width = x_ref.shape[2]

    weights = left_parts(m_ref[...])
    gate = jnp.concatenate([w_ref[...], w_ref[...]], axis=1)
    total = None
    for n in range(0, slabs, 2):
        high, low = [], []
        for k in (n, n + 1):
            rows = jnp.concatenate([x_ref[k], p_ref[k], q_ref[k], f_ref[k]], axis=0)
            hi, lo = halves(rows)
            high.append(hi)
            low.append(lo)
        high = jnp.concatenate(high, axis=1)
        low = jnp.concatenate(low, axis=1)
        both = jnp.concatenate([high, low], axis=0)
        out = jnp.dot(weights, both, preferred_element_type=f32)
        rows = out.shape[0] // 2
        out = out[:rows] + out[rows:]
        out = out[: rows // 2] + gate * out[rows // 2 :]
        own = jnp.concatenate([b_ref[n], b_ref[n + 1]], axis=1) + out[:part]
        other = jnp.concatenate([bp_ref[n], bp_ref[n + 1]], axis=1) + out[part:]
        for k in (0, 1):
            a_ref[n + k] = own[:, k * width : (k + 1) * width]
            y_ref[n + k] = out[part:, k * width : (k + 1) * width]
        hi, lo = halves(jnp.concatenate([own, other], axis=0))
        cross = lax.dot_general(
            both,
            jnp.concatenate([hi, lo], axis=0),
            ROWS_BY_ROWS,
            preferred_element_type=f32,
        )
        total = cross if total is None else total + cross
    c_ref[0] = folded(total)


def inner_terms(gate, weights, x, p, q, f, b, bp):
    count, part, width = x.shape
    slabs = 16
    block = pl.BlockSpec((slabs, part, width), lambda i: (i, 0, 0))
    return pl.pallas_call(
        functools.partial(inner_body, slabs),
        grid=(count // slabs,),
        in_specs=[whole(gate), whole(weights)] + [block] * 6,
        out_specs=[block, block, pl.BlockSpec((1, 4 * part, 2 * part), lambda i: (i, 0, 0))],
        out_shape=[
            jax.ShapeDtypeStruct(x.shape, f32),
            jax.ShapeDtypeStruct(x.shape, f32),
            jax.ShapeDtypeStruct((count // slabs, 4 * part, 2 * part), f32),
        ],
        compiler_params=pltpu.CompilerParams(vmem_limit_bytes=VMEM_LIMIT),
        cost_estimate=pl.CostEstimate(
            flops=count * 6 * 2 * 128 * 128 * 128, bytes_accessed=count * part * width * 4 * 8, transcendentals=0
        ),
    )(gate, weights, x, p, q, f, b, bp)


def line_device(
    initial, target, rates_small, rates_large, pattern_small, pattern_large,
    spare_small, spare_large, trigger_first, trigger_last,
):
    gen_small, exit_small, open_small = generator(rates_small, pattern_small)
    gen_large, exit_large, open_large = generator(rates_large, pattern_large)
    rim_one = jnp.sum(spare_small, axis=1)
    rim_two = jnp.sum(spare_large, axis=1)
    weight_first = trigger_first.astype(f32)
    weight_last = trigger_last.astype(f32)
    bound = jnp.sum(jnp.max(exit_small, axis=1)) + jnp.sum(jnp.max(exit_large, axis=1))
    bound = bound + jnp.max(weight_first) * jnp.max(rim_one) + jnp.max(weight_last) * jnp.max(rim_two)
    step_size = 1.0 / bound

    size_small, size_large = initial.shape[0], initial.shape[3]
    wide = lax.axis_size("wide")
    wide_pos = lax.axis_index("wide")
    place = lax.axis_index("narrow")
    deep = size_small // wide
    rows, part = initial.shape[1], initial.shape[2]

    spare_one = spare_small - jnp.diag(rim_one)
    mine = lax.dynamic_slice_in_dim(weight_first, wide_pos * deep, deep)
    mode_one = step_size * (gen_small[1][None] + mine[:, None, None] * spare_one[None])
    mode_one = mode_one.transpose(0, 2, 1)

    inner = (place == 1) | (place == 2)
    partner = jnp.where(place < 2, 1 - place, 5 - place)
    spare_two = spare_large - jnp.diag(rim_two)
    factor = jnp.where(inner, step_size, 0.0)
    places = jnp.concatenate(
        [jnp.arange(part) + block * part for block in (place, partner, 3 - place, 3 - partner)]
    )
    spread = (places[:, None] == jnp.arange(size_large)[None]).astype(f32)
    picked = functools.partial(jnp.einsum, "xr,rc,yc->xy", precision=highest)
    weights = factor * jnp.concatenate(
        [picked(spread, m, spread[: 2 * part]) for m in (gen_large[0], spare_two)], axis=1
    ).T
    gate = weight_last[None, :]

    xv = initial.reshape(wide, deep, rows, part, size_large)
    half = deep // 2

    def shift(value, pairs):
        return lax.ppermute(value, "narrow", pairs)

    def exchange(value):
        return lax.all_to_all(value, "wide", 0, 0, tiled=True)

    def after(value, *done):
        return lax.optimization_barrier((value,) + done)[0]

    xs = [xv[:, lo:hi].reshape(-1, part, size_large) for lo, hi in PIECES]
    ps, qs, fs = [], [], []
    for k in range(len(PIECES)):
        piece = xs[k] if k < 2 else after(xs[k], ps[k - 2])
        ps.append(shift(piece, TO_INNER))
        qs.append(shift(piece, INNER_SWAP))
        fs.append(shift(ps[k], INNER_SWAP))

    base = base_terms(initial, target, step_size * gen_small[0].T, step_size * gen_large[1])

    wide_x = [exchange(xv[:, :half])]
    first = after(wide_x[0], base, ps[0], qs[0])
    back = [exchange(one_terms(first, mode_one[:half]))]
    wide_x.append(exchange(after(xv[:, half:], back[0])))
    bases = []

    def add_base(k):
        lo, hi = PIECES[k]
        at = lo % half
        total = base.reshape(xv.shape)[:, lo:hi] + back[lo // half][:, at : at + hi - lo]
        bases.append(total.reshape(-1, part, size_large))

    back[0] = after(back[0], ps[1], qs[1])
    add_base(0)
    add_base(1)
    others = [shift(b, TO_INNER) for b in bases]
    second = after(wide_x[1], fs[0], ps[2], *bases)
    back.append(exchange(one_terms(second, mode_one[half:])))

    adjoints, wide_a, sums_two, own, far = [], [], [], [], []

    def inner_step(k, *done):
        b = after(bases[k], *done) if done else bases[k]
        a, y, c2 = inner_terms(gate, weights, xs[k], ps[k], qs[k], fs[k], b, others[k])
        sums_two.append(c2)
        own.append(a)
        far.append(shift(y, TO_OUTER))

    def finish(k, *done):
        a = after(own[k], *done) if done else own[k]
        lo, hi = PIECES[k]
        adjoints.append((a + far[k]).reshape(wide, hi - lo, rows, part, size_large))
        wide_a.append(exchange(adjoints[k]))

    inner_step(0)
    back[1] = after(back[1], own[0], qs[2])
    for k in (2, 3, 4):
        add_base(k)
        others.append(shift(bases[k], TO_INNER))
    finish(0, bases[2])
    inner_step(1, adjoints[0])
    finish(1, own[1])
    inner_step(2, adjoints[1])
    ones = []

    def cross_step(k, *done):
        a = after(wide_a[k], *done)
        lo, _ = PIECES[k]
        ones.append(one_cross(wide_x[lo // half], a, lo % half))

    cross_step(0, own[2])
    cross_step(1, ones[0])
    inner_step(3, ones[1])
    finish(2, own[3])
    inner_step(4, adjoints[2])
    finish(3, own[4])
    cross_step(2, adjoints[3])
    finish(4, ones[2])
    cross_zero, cross_three = local_cross(xv, adjoints)
    cross_step(3, cross_three)
    cross_step(4, ones[3])
    cross_one = jnp.sum(jnp.concatenate(ones, axis=0), axis=0)
    found = jnp.where(inner, jnp.sum(jnp.concatenate(sums_two, axis=0), axis=0), 0.0)
    cross_two = jnp.einsum("xr,xy,yc->rc", spread, found, spread[: 2 * part], precision=highest)

    packed = jnp.concatenate(
        [jnp.concatenate([cross_zero, cross_one], axis=1), cross_two, cross_three], axis=0
    )
    packed = all_sum(packed, ("wide", "narrow"))
    small = jnp.stack([packed[:size_small, :size_small], packed[:size_small, size_small:]])
    large = packed[size_small:].reshape(2, size_large, size_large)
    small = small / math.sqrt(size_small * size_large * size_large)
    large = large / math.sqrt(size_small * size_small * size_large)
    grad_small = open_small * (small - jnp.diagonal(small, axis1=1, axis2=2)[:, :, None])
    grad_large = open_large * (large - jnp.diagonal(large, axis1=1, axis2=2)[:, :, None])
    return (grad_small, grad_large)


def enter_first(tensor):
    return lax.all_to_all(tensor, "wide", split_axis=0, concat_axis=1, tiled=True)


def leave_first(tensor):
    return lax.all_to_all(tensor, "wide", split_axis=1, concat_axis=0, tiled=True)


def enter_second(tensor):
    return lax.all_to_all(tensor, "narrow", split_axis=0, concat_axis=2, tiled=True)


def leave_second(tensor):
    return lax.all_to_all(tensor, "narrow", split_axis=2, concat_axis=0, tiled=True)


def rearranged(tensor):
    return (enter_first(tensor), enter_second(tensor))


def local_part(tensor, mode_zero, mode_three):
    local_terms = jnp.einsum("abcd,ae->ebcd", tensor, mode_zero, precision=highest)
    return local_terms + jnp.einsum("abcd,de->abce", tensor, mode_three, precision=highest)


def operate(tensor, matrices, weights):
    mode_zero, mode_one, mode_two, mode_three, spare_one, spare_two, rim_one, rim_two = matrices
    weight_part, weight_last, weight_tail = weights
    local_terms = local_part(tensor, mode_zero, mode_three)
    tensor_wide = enter_first(tensor)
    tensor_narrow = enter_second(tensor)
    lifted = tensor_wide * weight_part[:, None, None, None]
    wide_terms = jnp.einsum("abcd,be->aecd", tensor_wide, mode_one, precision=highest)
    wide_terms = (
        wide_terms
        + jnp.einsum("abcd,be->aecd", lifted, spare_one, precision=highest)
        - lifted * rim_one[None, :, None, None]
    )
    lowered = tensor_narrow * weight_last[None, None, None, :]
    narrow_terms = jnp.einsum("abcd,ce->abed", tensor_narrow, mode_two, precision=highest)
    narrow_terms = (
        narrow_terms
        + jnp.einsum("abcd,ce->abed", lowered, spare_two, precision=highest)
        - lowered * rim_two[None, None, :, None]
    )
    return (
        local_terms + leave_first(wide_terms) + leave_second(narrow_terms),
        tensor_wide,
        tensor_narrow,
    )


def cross_terms(state_prev, adjoint_now, state_wide, adjoint_wide, state_narrow, adjoint_narrow):
    cross_zero = jnp.einsum("abcd,ebcd->ae", state_prev, adjoint_now, precision=highest)
    cross_three = jnp.einsum("abcd,abce->de", state_prev, adjoint_now, precision=highest)
    cross_one = jnp.einsum("abcd,aecd->be", state_wide, adjoint_wide, precision=highest)
    cross_two = jnp.einsum("abcd,abed->ce", state_narrow, adjoint_narrow, precision=highest)
    return (jnp.stack([cross_zero, cross_one]), jnp.stack([cross_two, cross_three]))


def on_device(
    initial,
    target,
    rates_small,
    rates_large,
    pattern_small,
    pattern_large,
    spare_small,
    spare_large,
    trigger_first,
    trigger_last,
):
    gen_small, exit_small, open_small = generator(rates_small, pattern_small)
    gen_large, exit_large, open_large = generator(rates_large, pattern_large)
    rim_one = jnp.sum(spare_small, axis=1)
    rim_two = jnp.sum(spare_large, axis=1)
    weight_first = trigger_first.astype(jnp.float32)
    weight_last = trigger_last.astype(jnp.float32)
    bound = jnp.sum(jnp.max(exit_small, axis=1)) + jnp.sum(jnp.max(exit_large, axis=1))
    bound = (
        bound + jnp.max(weight_first) * jnp.max(rim_one) + jnp.max(weight_last) * jnp.max(rim_two)
    )
    step_size = 1.0 / bound
    wide_pos = lax.axis_index("wide")
    rows_wide = initial.shape[0] // lax.axis_size("wide")
    weight_part = lax.dynamic_slice_in_dim(weight_first, wide_pos * rows_wide, rows_wide)
    narrow_pos = lax.axis_index("narrow")
    rows_narrow = initial.shape[3] // lax.axis_size("narrow")
    weight_tail = lax.dynamic_slice_in_dim(weight_last, narrow_pos * rows_narrow, rows_narrow)
    weights = (weight_part, weight_last, weight_tail)
    onward = (
        gen_small[0],
        gen_small[1],
        gen_large[0],
        gen_large[1],
        spare_small,
        spare_large,
        rim_one,
        rim_two,
    )
    new_terms, start_wide, start_narrow = operate(initial, onward, weights)
    state = initial + step_size * new_terms
    adjoint = state - target
    adjoint_wide, adjoint_narrow = rearranged(adjoint)
    again_wide, again_narrow = rearranged(initial)
    terms = cross_terms(initial, adjoint, again_wide, adjoint_wide, again_narrow, adjoint_narrow)
    small, large = lax.psum((terms[0], terms[1]), ("wide", "narrow"))
    size_small = initial.shape[0]
    size_large = initial.shape[3]
    small = small / math.sqrt(size_small * size_large * size_large)
    large = large / math.sqrt(size_small * size_small * size_large)
    grad_small = open_small * (small - jnp.diagonal(small, axis1=1, axis2=2)[:, :, None])
    grad_large = open_large * (large - jnp.diagonal(large, axis1=1, axis2=2)[:, :, None])
    return (grad_small, grad_large)


def solution(mesh):
    line = mesh.shape["narrow"] == 4 and mesh.shape["wide"] == 8
    return jax.shard_map(
        line_device if line else on_device,
        mesh=mesh,
        in_specs=(
            P(None, "wide", "narrow", None),
            P(None, "wide", "narrow", None),
            P(),
            P(),
            P(),
            P(),
            P(),
            P(),
            P(),
            P(),
        ),
        out_specs=(P(), P()),
        check_vma=False,
    )
```

```python
import functools
import math

import jax
import jax.numpy as jnp
from jax import lax
from jax.experimental import pallas as pl
from jax.experimental.pallas import tpu as pltpu
from jax.sharding import PartitionSpec as P

highest = lax.Precision.HIGHEST
f32 = jnp.float32
VMEM_LIMIT = 40 * 1024 * 1024
bf16 = jnp.bfloat16

TO_INNER = [(0, 1), (3, 2)]
INNER_SWAP = [(1, 2), (2, 1)]
TO_OUTER = [(1, 0), (2, 3)]

PIECES = [(0, 2), (2, 4), (4, 6), (6, 7), (7, 8)]

ROWS_BY_ROWS = (((1,), (1,)), ((), ()))
DEPTH_BY_DEPTH = (((0,), (0,)), ((), ()))


def generator(rate_matrix, pattern):
    extent = rate_matrix.shape[-1]
    identity = jnp.eye(extent, dtype=jnp.float32)
    opened = pattern.astype(jnp.float32) * (1.0 - identity)
    flow_rates = rate_matrix * opened
    leaving = jnp.sum(flow_rates, axis=-1)
    return (flow_rates - leaving[..., :, None] * identity, leaving, opened)


def halves(value):
    high = value.astype(bf16)
    low = (value - high.astype(f32)).astype(bf16)
    return high, low


def all_sum(value, axes):
    for axis in axes:
        extent = lax.axis_size(axis)
        step = 1
        while step < extent:
            pairs = [(i, i ^ step) for i in range(extent)]
            value = value + lax.ppermute(value, axis, pairs)
            step *= 2
    return value


def run(body, grid, in_specs, out_specs, out_shape, args, done):
    count, extra = len(args), len(done)

    def kernel(*refs):
        body(*refs[:count], *refs[count + extra :])

    return pl.pallas_call(
        kernel,
        grid=grid,
        in_specs=list(in_specs) + [pl.BlockSpec(memory_space=pltpu.HBM)] * extra,
        out_specs=out_specs,
        out_shape=out_shape,
        compiler_params=pltpu.CompilerParams(vmem_limit_bytes=VMEM_LIMIT),
        cost_estimate=pl.CostEstimate(flops=0, bytes_accessed=0, transcendentals=0),
    )(*args, *done)


def whole(array):
    return pl.BlockSpec(array.shape, lambda i: (0,) * array.ndim)


def stacked_rows(ref, count, inner, at):
    rows = [ref[pl.ds(at + k, count, stride=inner), :] for k in (0, 1)]
    high, low = halves(jnp.concatenate(rows, axis=1))
    return jnp.concatenate([high, low], axis=0)


def left_parts(matrix):
    high, low = halves(matrix)
    return jnp.concatenate(
        [jnp.concatenate([high, high], axis=1), jnp.concatenate([low, low], axis=1)], axis=0
    )


def folded(total):
    rows, cols = total.shape[0] // 2, total.shape[1] // 2
    total = total[:rows] + total[rows:]
    return total[:, :cols] + total[:, cols:]


def product(matrix, in_ref, out_ref, count, inner, add):
    width = in_ref.shape[1]
    for at in range(0, inner, 2):
        out = jnp.dot(matrix, stacked_rows(in_ref, count, inner, at), preferred_element_type=f32)
        out = out[:count] + out[count:]
        for k in (0, 1):
            place = pl.ds(at + k, count, stride=inner)
            piece = out[:, k * width : (k + 1) * width]
            out_ref[place, :] = out_ref[place, :] + piece if add else piece


def base_body(x_ref, t_ref, first_ref, last_ref, o_ref):
    count, _, inner, width = x_ref.shape
    x2, t2, o2 = (ref.reshape(count * inner, width) for ref in (x_ref, t_ref, o_ref))
    high, low = halves(last_ref[...])
    last = jnp.concatenate([jnp.concatenate([high, low], axis=1)] * 2, axis=0)
    for r in range(0, count * inner, 256):
        x = x2[r : r + 256]
        high, low = halves(x)
        out = jnp.dot(jnp.concatenate([high, low], axis=1), last, preferred_element_type=f32)
        o2[r : r + 256] = x - t2[r : r + 256] + (out[:, :width] + out[:, width:])
    product(left_parts(first_ref[...]), x2, o2, count, inner, True)


def base_terms(x, t, first, last, *done):
    block = pl.BlockSpec((x.shape[0], 1) + x.shape[2:], lambda i: (0, i, 0, 0))
    return run(
        base_body,
        (x.shape[1],),
        [block, block, whole(first), whole(last)],
        block,
        jax.ShapeDtypeStruct(x.shape, f32),
        (x, t, first, last,),
        done,
    )


def one_body(x_ref, k_ref, o_ref):
    blocks, _, rows, inner, width = x_ref.shape
    count = blocks * rows
    x2, o2 = x_ref.reshape(count * inner, width), o_ref.reshape(count * inner, width)
    product(left_parts(k_ref[0]), x2, o2, count, inner, False)


def one_terms(x, matrices, skip, states, *done):
    block = lambda skip: pl.BlockSpec((x.shape[0], 1) + x.shape[2:], lambda i: (0, i + skip, 0, 0, 0))
    return run(
        one_body,
        (states,),
        [block(skip), pl.BlockSpec((1,) + matrices.shape[1:], lambda i: (i + skip, 0, 0))],
        block(0),
        jax.ShapeDtypeStruct((x.shape[0], states) + x.shape[2:], f32),
        (x, matrices,),
        done,
    )


def one_cross_body(x_ref, a_ref, o_ref):
    blocks, _, rows, inner, width = x_ref.shape
    count = blocks * rows
    x2, a2 = x_ref.reshape(count * inner, width), a_ref.reshape(count * inner, width)
    total = None
    for at in range(0, inner, 2):
        term = lax.dot_general(
            stacked_rows(x2, count, inner, at),
            stacked_rows(a2, count, inner, at),
            ROWS_BY_ROWS,
            preferred_element_type=f32,
        )
        total = term if total is None else total + term
    o_ref[0] = folded(total)


def one_cross(x, a, skip, *done):
    count = x.shape[0] * x.shape[2]
    shape = (x.shape[0], 1) + x.shape[2:]
    out = run(
        one_cross_body,
        (a.shape[1],),
        [
            pl.BlockSpec(shape, lambda i: (0, i + skip, 0, 0, 0)),
            pl.BlockSpec(shape, lambda i: (0, i, 0, 0, 0)),
        ],
        pl.BlockSpec((1, count, count), lambda i: (i, 0, 0)),
        jax.ShapeDtypeStruct((a.shape[1], count, count), f32),
        (x, a,),
        done,
    )
    return out


def local_body(pieces, x_ref, *refs):
    a_refs, o_ref, o3_ref = refs[: len(pieces)], refs[-2], refs[-1]
    wide, deep, _, inner, width = x_ref.shape
    x2 = x_ref.reshape(wide * deep * inner, width)
    flat = [a.reshape(a.shape[0] * a.shape[1] * inner, width) for a in a_refs]
    total = None
    for at in range(0, inner, 2):
        parts = []
        for k in (0, 1):
            rows = [
                a[pl.ds(at + k, wide * (hi - lo), stride=inner), :] for a, (lo, hi) in zip(flat, pieces)
            ]
            parts.append(jnp.concatenate(rows, axis=0))
        high, low = halves(jnp.concatenate(parts, axis=1))
        term = lax.dot_general(
            stacked_rows(x2, wide * deep, inner, at),
            jnp.concatenate([high, low], axis=0),
            ROWS_BY_ROWS,
            preferred_element_type=f32,
        )
        total = term if total is None else total + term
    o_ref[0] = folded(total)
    total = None
    for a_ref, (lo, hi) in zip(a_refs, pieces):
        for s in range(lo, hi):
            sides = []
            for ref, at in ((x_ref, s), (a_ref, s - lo)):
                rows = jnp.concatenate([ref[w, at, 0] for w in range(wide)], axis=0)
                sides.append(jnp.concatenate(halves(rows), axis=1))
            term = lax.dot_general(sides[0], sides[1], DEPTH_BY_DEPTH, preferred_element_type=f32)
            total = term if total is None else total + term
    o3_ref[0] = folded(total)


def local_cross(x, adjoints, *done):
    wide, deep, rows, inner, width = x.shape
    block = lambda a: pl.BlockSpec((wide, a.shape[1], 1, inner, width), lambda i: (0, 0, i, 0, 0))
    count = wide * deep
    zero, three = run(
        functools.partial(local_body, PIECES),
        (rows,),
        [block(x)] + [block(a) for a in adjoints],
        [
            pl.BlockSpec((1, count, count), lambda i: (i, 0, 0)),
            pl.BlockSpec((1, width, width), lambda i: (i, 0, 0)),
        ],
        [
            jax.ShapeDtypeStruct((rows, count, count), f32),
            jax.ShapeDtypeStruct((rows, width, width), f32),
        ],
        (x, *adjoints,),
        done,
    )
    zero = jnp.sum(zero, axis=0)
    columns, at = [], 0
    for lo, hi in PIECES:
        size = wide * (hi - lo)
        columns.append(zero[:, at : at + size].reshape(count, wide, hi - lo))
        at += size
    zero = jnp.concatenate(columns, axis=2).reshape(count, count)
    return zero, jnp.sum(three, axis=0)


def block_pair(refs, n):
    sides = [jnp.concatenate([ref[k] for ref in refs], axis=0) for k in (n, n + 1)]
    high, low = halves(jnp.concatenate(sides, axis=1))
    return jnp.concatenate([high, low], axis=0)


def pair_terms_body(w_ref, m_ref, x_ref, p_ref, q_ref, f_ref, own_ref, other_ref):
    cells, part, width = x_ref.shape
    weights = left_parts(m_ref[...])
    gate = jnp.concatenate([w_ref[...], w_ref[...]], axis=1)
    for n in range(0, cells, 2):
        both = block_pair((x_ref, p_ref, q_ref, f_ref), n)
        out = jnp.dot(weights, both, preferred_element_type=f32)
        rows = out.shape[0] // 2
        out = out[:rows] + out[rows:]
        out = out[: rows // 2] + gate * out[rows // 2 :]
        for k in (0, 1):
            own_ref[n + k] = out[:part, k * width : (k + 1) * width]
            other_ref[n + k] = out[part:, k * width : (k + 1) * width]


def pair_cross_body(x_ref, p_ref, q_ref, f_ref, own_ref, base_ref, terms_ref, c_ref):
    total = None
    for n in range(0, x_ref.shape[0], 2):
        sides = [
            jnp.concatenate([own_ref[k], base_ref[k] + terms_ref[k]], axis=0) for k in (n, n + 1)
        ]
        high, low = halves(jnp.concatenate(sides, axis=1))
        term = lax.dot_general(
            block_pair((x_ref, p_ref, q_ref, f_ref), n),
            jnp.concatenate([high, low], axis=0),
            ROWS_BY_ROWS,
            preferred_element_type=f32,
        )
        total = term if total is None else total + term
    c_ref[0] = folded(total)


def pair_terms(gate, weights, blocks, *done):
    count, part, width = blocks[0].shape
    cells = 16
    block = pl.BlockSpec((cells, part, width), lambda i: (i, 0, 0))
    return run(
        pair_terms_body,
        (count // cells,),
        [whole(gate), whole(weights)] + [block] * 4,
        [block, block],
        [jax.ShapeDtypeStruct(blocks[0].shape, f32)] * 2,
        (gate, weights, *blocks,),
        done,
    )


def pair_cross(blocks, *done):
    count, part, width = blocks[0].shape
    cells = 16
    block = pl.BlockSpec((cells, part, width), lambda i: (i, 0, 0))
    shape = (count // cells, 4 * part, 2 * part)
    return run(
        pair_cross_body,
        (count // cells,),
        [block] * 7,
        pl.BlockSpec((1,) + shape[1:], lambda i: (i, 0, 0)),
        jax.ShapeDtypeStruct(shape, f32),
        (*blocks,),
        done,
    )


def copy_body(x_ref, o_ref):
    o_ref[...] = x_ref[...]


def sum_body(*refs):
    total = refs[0][...]
    for ref in refs[1:-1]:
        total = total + ref[...]
    refs[-1][...] = total


def piece_of(lo, hi, skip, shape):
    size = hi - lo
    return pl.BlockSpec((1, size) + shape[2:], lambda i: (i, (lo - skip) // size, 0, 0, 0))


def cut_piece(x, lo, hi, *done):
    out = jax.ShapeDtypeStruct((x.shape[0], hi - lo) + x.shape[2:], f32)
    return run(
        copy_body, (x.shape[0],), [piece_of(lo, hi, 0, x.shape)], piece_of(lo, hi, lo, x.shape), out, (x,), done
    )


def add_piece(x, y, skip, lo, hi, *done):
    out = jax.ShapeDtypeStruct((x.shape[0], hi - lo) + x.shape[2:], f32)
    return run(
        sum_body,
        (x.shape[0],),
        [piece_of(lo, hi, 0, x.shape), piece_of(lo, hi, skip, x.shape)],
        piece_of(lo, hi, lo, x.shape),
        out,
        (x, y),
        done,
    )


def add_all(arrays, *done):
    shape = arrays[0].shape
    block = pl.BlockSpec((shape[0] // 4,) + shape[1:], lambda i: (i, 0, 0))
    out = jax.ShapeDtypeStruct(shape, f32)
    return run(sum_body, (4,), [block] * len(arrays), block, out, tuple(arrays), done)


def line_device(
    initial, target, rates_small, rates_large, pattern_small, pattern_large,
    spare_small, spare_large, trigger_first, trigger_last,
):
    gen_small, exit_small, open_small = generator(rates_small, pattern_small)
    gen_large, exit_large, open_large = generator(rates_large, pattern_large)
    rim_one = jnp.sum(spare_small, axis=1)
    rim_two = jnp.sum(spare_large, axis=1)
    weight_first = trigger_first.astype(f32)
    weight_last = trigger_last.astype(f32)
    bound = jnp.sum(jnp.max(exit_small, axis=1)) + jnp.sum(jnp.max(exit_large, axis=1))
    bound = bound + jnp.max(weight_first) * jnp.max(rim_one) + jnp.max(weight_last) * jnp.max(rim_two)
    step_size = 1.0 / bound

    size_small, size_large = initial.shape[0], initial.shape[3]
    wide = lax.axis_size("wide")
    wide_pos = lax.axis_index("wide")
    place = lax.axis_index("narrow")
    deep = size_small // wide
    rows, part = initial.shape[1], initial.shape[2]

    spare_one = spare_small - jnp.diag(rim_one)
    mine = lax.dynamic_slice_in_dim(weight_first, wide_pos * deep, deep)
    mode_one = step_size * (gen_small[1][None] + mine[:, None, None] * spare_one[None])
    mode_one = mode_one.transpose(0, 2, 1)

    inner = (place == 1) | (place == 2)
    partner = jnp.where(place < 2, 1 - place, 5 - place)
    spare_two = spare_large - jnp.diag(rim_two)
    factor = jnp.where(inner, step_size, 0.0)
    places = jnp.concatenate(
        [jnp.arange(part) + block * part for block in (place, partner, 3 - place, 3 - partner)]
    )
    spread = (places[:, None] == jnp.arange(size_large)[None]).astype(f32)
    picked = functools.partial(jnp.einsum, "xr,rc,yc->xy", precision=highest)
    weights = factor * jnp.concatenate(
        [picked(spread, m, spread[: 2 * part]) for m in (gen_large[0], spare_two)], axis=1
    ).T
    gate = weight_last[None, :]

    xv = initial.reshape(wide, deep, rows, part, size_large)
    half = deep // 2

    def shift(value, pairs):
        return lax.ppermute(value, "narrow", pairs)

    def exchange(value):
        return lax.all_to_all(value, "wide", 0, 0, tiled=True)

    count = len(PIECES)
    xs, ps, qs, fs = ([None] * count for _ in range(4))
    bases, others, own, other, far = ([None] * count for _ in range(5))
    adjoints, wide_a, ones, twos = ([None] * count for _ in range(4))

    def flat(value):
        return value.reshape(-1, part, size_large)

    def send_piece(k, *done):
        xs[k] = flat(cut_piece(xv, *PIECES[k], *done))
        ps[k] = shift(xs[k], TO_INNER)
        qs[k] = shift(xs[k], INNER_SWAP)
        fs[k] = shift(ps[k], INNER_SWAP)

    def base_step(k, *done):
        lo, hi = PIECES[k]
        bases[k] = flat(add_piece(base.reshape(xv.shape), back[lo // half], lo // half * half, lo, hi, *done))
        others[k] = shift(bases[k], TO_INNER)

    def terms_step(k, *done):
        own[k], other[k] = pair_terms(gate, weights, (xs[k], ps[k], qs[k], fs[k]), *done)
        far[k] = shift(other[k], TO_OUTER)

    def finish(k, *done):
        lo, hi = PIECES[k]
        total = add_all((own[k], far[k], bases[k]), *done)
        adjoints[k] = total.reshape(wide, hi - lo, rows, part, size_large)
        wide_a[k] = exchange(adjoints[k])

    def one_step(k, *done):
        ones[k] = one_cross(wide_x, wide_a[k], PIECES[k][0], *done)

    def two_step(k, *done):
        twos[k] = pair_cross((xs[k], ps[k], qs[k], fs[k], flat(adjoints[k]), others[k], other[k]), *done)

    wide_x = exchange(xv)
    send_piece(0)
    send_piece(1)
    for k in (2, 3, 4):
        send_piece(k, xs[1])
    base = base_terms(initial, target, step_size * gen_small[0].T, step_size * gen_large[1], xs[4])
    one_first = one_terms(wide_x, mode_one, 0, half, base, ps[0], qs[0], ps[1], qs[1])
    one_second = one_terms(wide_x, mode_one, half, deep - half, one_first)
    back = [exchange(one_first), exchange(one_second)]
    terms_step(0, one_second)
    base_step(0, own[0])
    base_step(1, bases[0])
    terms_step(1, bases[1], ps[2], ps[3], ps[4])
    base_step(2, own[1])
    base_step(3, bases[2])
    base_step(4, bases[3])
    finish(0, bases[4])
    terms_step(2, adjoints[0])
    finish(1, own[2])
    two_step(0, adjoints[1])
    two_step(1, twos[0])
    terms_step(3, twos[1])
    finish(2, own[3])
    one_step(0, adjoints[2])
    one_step(1, ones[0])
    two_step(2, ones[1])
    terms_step(4, twos[2])
    finish(3, own[4])
    one_step(2, adjoints[3])
    two_step(3, ones[2])
    finish(4, twos[3])
    cross_zero, cross_three = local_cross(xv, adjoints)
    two_step(4, cross_three)
    one_step(3, twos[4])
    one_step(4, ones[3])
    cross_one = jnp.sum(jnp.concatenate(ones, axis=0), axis=0)
    found = jnp.where(inner, jnp.sum(jnp.concatenate(twos, axis=0), axis=0), 0.0)
    cross_two = jnp.einsum("xr,xy,yc->rc", spread, found, spread[: 2 * part], precision=highest)

    packed = jnp.concatenate(
        [jnp.concatenate([cross_zero, cross_one], axis=1), cross_two, cross_three], axis=0
    )
    packed = all_sum(packed, ("wide", "narrow"))
    small = jnp.stack([packed[:size_small, :size_small], packed[:size_small, size_small:]])
    large = packed[size_small:].reshape(2, size_large, size_large)
    small = small / math.sqrt(size_small * size_large * size_large)
    large = large / math.sqrt(size_small * size_small * size_large)
    grad_small = open_small * (small - jnp.diagonal(small, axis1=1, axis2=2)[:, :, None])
    grad_large = open_large * (large - jnp.diagonal(large, axis1=1, axis2=2)[:, :, None])
    return (grad_small, grad_large)


def enter_first(tensor):
    return lax.all_to_all(tensor, "wide", split_axis=0, concat_axis=1, tiled=True)


def leave_first(tensor):
    return lax.all_to_all(tensor, "wide", split_axis=1, concat_axis=0, tiled=True)


def enter_second(tensor):
    return lax.all_to_all(tensor, "narrow", split_axis=0, concat_axis=2, tiled=True)


def leave_second(tensor):
    return lax.all_to_all(tensor, "narrow", split_axis=2, concat_axis=0, tiled=True)


def rearranged(tensor):
    return (enter_first(tensor), enter_second(tensor))


def local_part(tensor, mode_zero, mode_three):
    local_terms = jnp.einsum("abcd,ae->ebcd", tensor, mode_zero, precision=highest)
    return local_terms + jnp.einsum("abcd,de->abce", tensor, mode_three, precision=highest)


def operate(tensor, matrices, weights):
    mode_zero, mode_one, mode_two, mode_three, spare_one, spare_two, rim_one, rim_two = matrices
    weight_part, weight_last, weight_tail = weights
    local_terms = local_part(tensor, mode_zero, mode_three)
    tensor_wide = enter_first(tensor)
    tensor_narrow = enter_second(tensor)
    lifted = tensor_wide * weight_part[:, None, None, None]
    wide_terms = jnp.einsum("abcd,be->aecd", tensor_wide, mode_one, precision=highest)
    wide_terms = (
        wide_terms
        + jnp.einsum("abcd,be->aecd", lifted, spare_one, precision=highest)
        - lifted * rim_one[None, :, None, None]
    )
    lowered = tensor_narrow * weight_last[None, None, None, :]
    narrow_terms = jnp.einsum("abcd,ce->abed", tensor_narrow, mode_two, precision=highest)
    narrow_terms = (
        narrow_terms
        + jnp.einsum("abcd,ce->abed", lowered, spare_two, precision=highest)
        - lowered * rim_two[None, None, :, None]
    )
    return (
        local_terms + leave_first(wide_terms) + leave_second(narrow_terms),
        tensor_wide,
        tensor_narrow,
    )


def cross_terms(state_prev, adjoint_now, state_wide, adjoint_wide, state_narrow, adjoint_narrow):
    cross_zero = jnp.einsum("abcd,ebcd->ae", state_prev, adjoint_now, precision=highest)
    cross_three = jnp.einsum("abcd,abce->de", state_prev, adjoint_now, precision=highest)
    cross_one = jnp.einsum("abcd,aecd->be", state_wide, adjoint_wide, precision=highest)
    cross_two = jnp.einsum("abcd,abed->ce", state_narrow, adjoint_narrow, precision=highest)
    return (jnp.stack([cross_zero, cross_one]), jnp.stack([cross_two, cross_three]))


def on_device(
    initial,
    target,
    rates_small,
    rates_large,
    pattern_small,
    pattern_large,
    spare_small,
    spare_large,
    trigger_first,
    trigger_last,
):
    gen_small, exit_small, open_small = generator(rates_small, pattern_small)
    gen_large, exit_large, open_large = generator(rates_large, pattern_large)
    rim_one = jnp.sum(spare_small, axis=1)
    rim_two = jnp.sum(spare_large, axis=1)
    weight_first = trigger_first.astype(jnp.float32)
    weight_last = trigger_last.astype(jnp.float32)
    bound = jnp.sum(jnp.max(exit_small, axis=1)) + jnp.sum(jnp.max(exit_large, axis=1))
    bound = (
        bound + jnp.max(weight_first) * jnp.max(rim_one) + jnp.max(weight_last) * jnp.max(rim_two)
    )
    step_size = 1.0 / bound
    wide_pos = lax.axis_index("wide")
    rows_wide = initial.shape[0] // lax.axis_size("wide")
    weight_part = lax.dynamic_slice_in_dim(weight_first, wide_pos * rows_wide, rows_wide)
    narrow_pos = lax.axis_index("narrow")
    rows_narrow = initial.shape[3] // lax.axis_size("narrow")
    weight_tail = lax.dynamic_slice_in_dim(weight_last, narrow_pos * rows_narrow, rows_narrow)
    weights = (weight_part, weight_last, weight_tail)
    onward = (
        gen_small[0],
        gen_small[1],
        gen_large[0],
        gen_large[1],
        spare_small,
        spare_large,
        rim_one,
        rim_two,
    )
    new_terms, start_wide, start_narrow = operate(initial, onward, weights)
    state = initial + step_size * new_terms
    adjoint = state - target
    adjoint_wide, adjoint_narrow = rearranged(adjoint)
    again_wide, again_narrow = rearranged(initial)
    terms = cross_terms(initial, adjoint, again_wide, adjoint_wide, again_narrow, adjoint_narrow)
    small, large = lax.psum((terms[0], terms[1]), ("wide", "narrow"))
    size_small = initial.shape[0]
    size_large = initial.shape[3]
    small = small / math.sqrt(size_small * size_large * size_large)
    large = large / math.sqrt(size_small * size_small * size_large)
    grad_small = open_small * (small - jnp.diagonal(small, axis1=1, axis2=2)[:, :, None])
    grad_large = open_large * (large - jnp.diagonal(large, axis1=1, axis2=2)[:, :, None])
    return (grad_small, grad_large)


def solution(mesh):
    line = mesh.shape["narrow"] == 4 and mesh.shape["wide"] == 8
    return jax.shard_map(
        line_device if line else on_device,
        mesh=mesh,
        in_specs=(
            P(None, "wide", "narrow", None),
            P(None, "wide", "narrow", None),
            P(),
            P(),
            P(),
            P(),
            P(),
            P(),
            P(),
            P(),
        ),
        out_specs=(P(), P()),
        check_vma=False,
    )
```

```python
import functools
import math

import jax
import jax.numpy as jnp
from jax import lax
from jax.experimental import pallas as pl
from jax.experimental.pallas import tpu as pltpu
from jax.sharding import PartitionSpec as P

highest = lax.Precision.HIGHEST
f32 = jnp.float32
VMEM_LIMIT = 40 * 1024 * 1024
bf16 = jnp.bfloat16

TO_INNER = [(0, 1), (3, 2)]
INNER_SWAP = [(1, 2), (2, 1)]
TO_OUTER = [(1, 0), (2, 3)]

PIECES = [(0, 2), (2, 4), (4, 6), (6, 7), (7, 8)]

ROWS_BY_ROWS = (((1,), (1,)), ((), ()))
DEPTH_BY_DEPTH = (((0,), (0,)), ((), ()))


def generator(rate_matrix, pattern):
    extent = rate_matrix.shape[-1]
    identity = jnp.eye(extent, dtype=jnp.float32)
    opened = pattern.astype(jnp.float32) * (1.0 - identity)
    flow_rates = rate_matrix * opened
    leaving = jnp.sum(flow_rates, axis=-1)
    return (flow_rates - leaving[..., :, None] * identity, leaving, opened)


def halves(value):
    high = value.astype(bf16)
    low = (value - high.astype(f32)).astype(bf16)
    return high, low


def run(body, grid, in_specs, out_specs, out_shape, args, done, limit=VMEM_LIMIT):
    count, extra = len(args), len(done)

    def kernel(*refs):
        body(*refs[:count], *refs[count + extra :])

    return pl.pallas_call(
        kernel,
        grid=grid,
        in_specs=list(in_specs) + [pl.BlockSpec(memory_space=pltpu.HBM)] * extra,
        out_specs=out_specs,
        out_shape=out_shape,
        compiler_params=pltpu.CompilerParams(vmem_limit_bytes=limit),
        cost_estimate=pl.CostEstimate(flops=0, bytes_accessed=0, transcendentals=0),
    )(*args, *done)


def whole(array):
    return pl.BlockSpec(array.shape, lambda i: (0,) * array.ndim)


def stacked_rows(ref, count, inner, at):
    rows = [ref[pl.ds(at + k, count, stride=inner), :] for k in (0, 1)]
    high, low = halves(jnp.concatenate(rows, axis=1))
    return jnp.concatenate([high, low], axis=0)


def left_parts(matrix):
    high, low = halves(matrix)
    return jnp.concatenate(
        [jnp.concatenate([high, high], axis=1), jnp.concatenate([low, low], axis=1)], axis=0
    )


def folded(total):
    rows, cols = total.shape[0] // 2, total.shape[1] // 2
    total = total[:rows] + total[rows:]
    return total[:, :cols] + total[:, cols:]


def product(matrix, in_ref, out_ref, count, inner, add):
    width = in_ref.shape[1]
    for at in range(0, inner, 2):
        out = jnp.dot(matrix, stacked_rows(in_ref, count, inner, at), preferred_element_type=f32)
        out = out[:count] + out[count:]
        for k in (0, 1):
            place = pl.ds(at + k, count, stride=inner)
            piece = out[:, k * width : (k + 1) * width]
            out_ref[place, :] = out_ref[place, :] + piece if add else piece


def base_body(x_ref, t_ref, first_ref, last_ref, o_ref):
    count, _, inner, width = x_ref.shape
    x2, t2, o2 = (ref.reshape(count * inner, width) for ref in (x_ref, t_ref, o_ref))
    high, low = halves(last_ref[...])
    last = jnp.concatenate([jnp.concatenate([high, low], axis=1)] * 2, axis=0)
    for r in range(0, count * inner, 256):
        x = x2[r : r + 256]
        high, low = halves(x)
        out = jnp.dot(jnp.concatenate([high, low], axis=1), last, preferred_element_type=f32)
        o2[r : r + 256] = x - t2[r : r + 256] + (out[:, :width] + out[:, width:])
    product(left_parts(first_ref[...]), x2, o2, count, inner, True)


def base_terms(x, t, first, last, *done):
    block = pl.BlockSpec((x.shape[0], 1) + x.shape[2:], lambda i: (0, i, 0, 0))
    return run(
        base_body,
        (x.shape[1],),
        [block, block, whole(first), whole(last)],
        block,
        jax.ShapeDtypeStruct(x.shape, f32),
        (x, t, first, last,),
        done,
    )


def one_body(x_ref, k_ref, o_ref):
    blocks, _, rows, inner, width = x_ref.shape
    count = blocks * rows
    x2, o2 = x_ref.reshape(count * inner, width), o_ref.reshape(count * inner, width)
    product(left_parts(k_ref[0]), x2, o2, count, inner, False)


def one_terms(x, matrices, skip, states, *done):
    block = lambda skip: pl.BlockSpec((x.shape[0], 1) + x.shape[2:], lambda i: (0, i + skip, 0, 0, 0))
    return run(
        one_body,
        (states,),
        [block(skip), pl.BlockSpec((1,) + matrices.shape[1:], lambda i: (i + skip, 0, 0))],
        block(0),
        jax.ShapeDtypeStruct((x.shape[0], states) + x.shape[2:], f32),
        (x, matrices,),
        done,
    )


def one_cross_body(x_ref, a_ref, o_ref):
    blocks, _, rows, inner, width = x_ref.shape
    count = blocks * rows
    x2, a2 = x_ref.reshape(count * inner, width), a_ref.reshape(count * inner, width)
    total = None
    for at in range(0, inner, 2):
        term = lax.dot_general(
            stacked_rows(x2, count, inner, at),
            stacked_rows(a2, count, inner, at),
            ROWS_BY_ROWS,
            preferred_element_type=f32,
        )
        total = term if total is None else total + term
    o_ref[0] = folded(total)


def one_cross(x, a, skip, *done):
    count = x.shape[0] * x.shape[2]
    shape = (x.shape[0], 1) + x.shape[2:]
    out = run(
        one_cross_body,
        (a.shape[1],),
        [
            pl.BlockSpec(shape, lambda i: (0, i + skip, 0, 0, 0)),
            pl.BlockSpec(shape, lambda i: (0, i, 0, 0, 0)),
        ],
        pl.BlockSpec((1, count, count), lambda i: (i, 0, 0)),
        jax.ShapeDtypeStruct((a.shape[1], count, count), f32),
        (x, a,),
        done,
    )
    return out


def local_body(pieces, x_ref, *refs):
    a_refs, o_ref, o3_ref = refs[: len(pieces)], refs[-2], refs[-1]
    wide, deep, _, inner, width = x_ref.shape
    x2 = x_ref.reshape(wide * deep * inner, width)
    flat = [a.reshape(a.shape[0] * a.shape[1] * inner, width) for a in a_refs]
    total = None
    for at in range(0, inner, 2):
        parts = []
        for k in (0, 1):
            rows = [
                a[pl.ds(at + k, wide * (hi - lo), stride=inner), :] for a, (lo, hi) in zip(flat, pieces)
            ]
            parts.append(jnp.concatenate(rows, axis=0))
        high, low = halves(jnp.concatenate(parts, axis=1))
        term = lax.dot_general(
            stacked_rows(x2, wide * deep, inner, at),
            jnp.concatenate([high, low], axis=0),
            ROWS_BY_ROWS,
            preferred_element_type=f32,
        )
        total = term if total is None else total + term
    o_ref[0] = folded(total)
    total = None
    for a_ref, (lo, hi) in zip(a_refs, pieces):
        for s in range(lo, hi):
            sides = []
            for ref, at in ((x_ref, s), (a_ref, s - lo)):
                rows = jnp.concatenate([ref[w, at, 0] for w in range(wide)], axis=0)
                sides.append(jnp.concatenate(halves(rows), axis=1))
            term = lax.dot_general(sides[0], sides[1], DEPTH_BY_DEPTH, preferred_element_type=f32)
            total = term if total is None else total + term
    o3_ref[0] = folded(total)


def local_cross(x, adjoints, *done):
    wide, deep, rows, inner, width = x.shape
    block = lambda a: pl.BlockSpec((wide, a.shape[1], 1, inner, width), lambda i: (0, 0, i, 0, 0))
    count = wide * deep
    zero, three = run(
        functools.partial(local_body, PIECES),
        (rows,),
        [block(x)] + [block(a) for a in adjoints],
        [
            pl.BlockSpec((1, count, count), lambda i: (i, 0, 0)),
            pl.BlockSpec((1, width, width), lambda i: (i, 0, 0)),
        ],
        [
            jax.ShapeDtypeStruct((rows, count, count), f32),
            jax.ShapeDtypeStruct((rows, width, width), f32),
        ],
        (x, *adjoints,),
        done,
        56 * 1024 * 1024,
    )
    zero = jnp.sum(zero, axis=0)
    columns, at = [], 0
    for lo, hi in PIECES:
        size = wide * (hi - lo)
        columns.append(zero[:, at : at + size].reshape(count, wide, hi - lo))
        at += size
    zero = jnp.concatenate(columns, axis=2).reshape(count, count)
    return zero, jnp.sum(three, axis=0)


def block_pair(refs, n):
    sides = [jnp.concatenate([ref[k] for ref in refs], axis=0) for k in (n, n + 1)]
    high, low = halves(jnp.concatenate(sides, axis=1))
    return jnp.concatenate([high, low], axis=0)


def pair_terms_body(w_ref, m_ref, x_ref, p_ref, q_ref, f_ref, own_ref, other_ref):
    cells, part, width = x_ref.shape
    weights = left_parts(m_ref[...])
    gate = jnp.concatenate([w_ref[...], w_ref[...]], axis=1)
    for n in range(0, cells, 2):
        both = block_pair((x_ref, p_ref, q_ref, f_ref), n)
        out = jnp.dot(weights, both, preferred_element_type=f32)
        rows = out.shape[0] // 2
        out = out[:rows] + out[rows:]
        out = out[: rows // 2] + gate * out[rows // 2 :]
        for k in (0, 1):
            own_ref[n + k] = out[:part, k * width : (k + 1) * width]
            other_ref[n + k] = out[part:, k * width : (k + 1) * width]


def pair_cross_body(x_ref, p_ref, q_ref, f_ref, b_ref, own_ref, base_ref, terms_ref, c_ref):
    total = None
    for n in range(0, x_ref.shape[0], 2):
        sides = [
            jnp.concatenate([b_ref[k] + own_ref[k], base_ref[k] + terms_ref[k]], axis=0) for k in (n, n + 1)
        ]
        high, low = halves(jnp.concatenate(sides, axis=1))
        term = lax.dot_general(
            block_pair((x_ref, p_ref, q_ref, f_ref), n),
            jnp.concatenate([high, low], axis=0),
            ROWS_BY_ROWS,
            preferred_element_type=f32,
        )
        total = term if total is None else total + term
    c_ref[0] = folded(total)


def pair_terms(gate, weights, blocks, *done):
    count, part, width = blocks[0].shape
    cells = 16
    block = pl.BlockSpec((cells, part, width), lambda i: (i, 0, 0))
    return run(
        pair_terms_body,
        (count // cells,),
        [whole(gate), whole(weights)] + [block] * 4,
        [block, block],
        [jax.ShapeDtypeStruct(blocks[0].shape, f32)] * 2,
        (gate, weights, *blocks,),
        done,
    )


def pair_cross(blocks, *done):
    count, part, width = blocks[0].shape
    cells = 16
    block = pl.BlockSpec((cells, part, width), lambda i: (i, 0, 0))
    shape = (count // cells, 4 * part, 2 * part)
    return run(
        pair_cross_body,
        (count // cells,),
        [block] * 8,
        pl.BlockSpec((1,) + shape[1:], lambda i: (i, 0, 0)),
        jax.ShapeDtypeStruct(shape, f32),
        (*blocks,),
        done,
    )


def last_body(scale_small, scale_large, a_ref, b_ref, small_ref, large_ref, s_ref, l_ref):
    total = a_ref[...] + b_ref[...]

    def gradient(cross, opened):
        same = lax.broadcasted_iota(jnp.int32, cross.shape, 0) == lax.broadcasted_iota(jnp.int32, cross.shape, 1)
        diagonal = jnp.sum(jnp.where(same, cross, 0.0), axis=1, keepdims=True)
        return opened * (cross - diagonal)

    small, large = s_ref.shape[1], l_ref.shape[1]
    for k in (0, 1):
        cross = total[:small, k * small : (k + 1) * small] / scale_small
        s_ref[k] = gradient(cross, small_ref[k])
        cross = total[small + k * large : small + (k + 1) * large] / scale_large
        l_ref[k] = gradient(cross, large_ref[k])


def copy_body(x_ref, o_ref):
    o_ref[...] = x_ref[...]


def sum_body(*refs):
    total = refs[0][...]
    for ref in refs[1:-1]:
        total = total + ref[...]
    refs[-1][...] = total


def piece_of(lo, hi, skip, shape):
    size = hi - lo
    return pl.BlockSpec((1, size) + shape[2:], lambda i: (i, (lo - skip) // size, 0, 0, 0))


def cut_piece(x, lo, hi, *done):
    out = jax.ShapeDtypeStruct((x.shape[0], hi - lo) + x.shape[2:], f32)
    return run(
        copy_body, (x.shape[0],), [piece_of(lo, hi, 0, x.shape)], piece_of(lo, hi, lo, x.shape), out, (x,), done
    )


def add_piece(x, y, skip, lo, hi, *done):
    out = jax.ShapeDtypeStruct((x.shape[0], hi - lo) + x.shape[2:], f32)
    return run(
        sum_body,
        (x.shape[0],),
        [piece_of(lo, hi, 0, x.shape), piece_of(lo, hi, skip, x.shape)],
        piece_of(lo, hi, lo, x.shape),
        out,
        (x, y),
        done,
    )


def add_all(arrays, *done):
    shape = arrays[0].shape
    block = pl.BlockSpec((shape[0] // 4,) + shape[1:], lambda i: (i, 0, 0))
    out = jax.ShapeDtypeStruct(shape, f32)
    return run(sum_body, (4,), [block] * len(arrays), block, out, tuple(arrays), done)


def line_device(
    initial, target, rates_small, rates_large, pattern_small, pattern_large,
    spare_small, spare_large, trigger_first, trigger_last,
):
    gen_small, exit_small, open_small = generator(rates_small, pattern_small)
    gen_large, exit_large, open_large = generator(rates_large, pattern_large)
    rim_one = jnp.sum(spare_small, axis=1)
    rim_two = jnp.sum(spare_large, axis=1)
    weight_first = trigger_first.astype(f32)
    weight_last = trigger_last.astype(f32)
    bound = jnp.sum(jnp.max(exit_small, axis=1)) + jnp.sum(jnp.max(exit_large, axis=1))
    bound = bound + jnp.max(weight_first) * jnp.max(rim_one) + jnp.max(weight_last) * jnp.max(rim_two)
    step_size = 1.0 / bound

    size_small, size_large = initial.shape[0], initial.shape[3]
    wide = lax.axis_size("wide")
    wide_pos = lax.axis_index("wide")
    place = lax.axis_index("narrow")
    deep = size_small // wide
    rows, part = initial.shape[1], initial.shape[2]

    spare_one = spare_small - jnp.diag(rim_one)
    mine = lax.dynamic_slice_in_dim(weight_first, wide_pos * deep, deep)
    mode_one = step_size * (gen_small[1][None] + mine[:, None, None] * spare_one[None])
    mode_one = mode_one.transpose(0, 2, 1)

    inner = (place == 1) | (place == 2)
    partner = jnp.where(place < 2, 1 - place, 5 - place)
    spare_two = spare_large - jnp.diag(rim_two)
    factor = jnp.where(inner, step_size, 0.0)
    places = jnp.concatenate(
        [jnp.arange(part) + block * part for block in (place, partner, 3 - place, 3 - partner)]
    )
    spread = (places[:, None] == jnp.arange(size_large)[None]).astype(f32)
    picked = functools.partial(jnp.einsum, "xr,rc,yc->xy", precision=highest)
    weights = factor * jnp.concatenate(
        [picked(spread, m, spread[: 2 * part]) for m in (gen_large[0], spare_two)], axis=1
    ).T
    gate = weight_last[None, :]

    xv = initial.reshape(wide, deep, rows, part, size_large)
    half = deep // 2

    def shift(value, pairs):
        return lax.ppermute(value, "narrow", pairs)

    def exchange(value):
        return lax.all_to_all(value, "wide", 0, 0, tiled=True)

    count = len(PIECES)
    xs, ps, qs, fs = ([None] * count for _ in range(4))
    bases, others, own, other, far = ([None] * count for _ in range(5))
    adjoints, wide_a, ones, twos = ([None] * count for _ in range(4))

    def flat(value):
        return value.reshape(-1, part, size_large)

    def send_piece(k, *done):
        xs[k] = flat(cut_piece(xv, *PIECES[k], *done))
        ps[k] = shift(xs[k], TO_INNER)
        qs[k] = shift(xs[k], INNER_SWAP)
        fs[k] = shift(ps[k], INNER_SWAP)

    def base_step(k, *done):
        lo, hi = PIECES[k]
        bases[k] = flat(add_piece(base.reshape(xv.shape), back[lo // half], lo // half * half, lo, hi, *done))
        others[k] = shift(bases[k], TO_INNER)

    def terms_step(k, *done):
        own[k], other[k] = pair_terms(gate, weights, (xs[k], ps[k], qs[k], fs[k]), *done)
        far[k] = shift(other[k], TO_OUTER)

    def finish(k, *done):
        lo, hi = PIECES[k]
        total = add_all((own[k], far[k], bases[k]), *done)
        adjoints[k] = total.reshape(wide, hi - lo, rows, part, size_large)
        wide_a[k] = exchange(adjoints[k])

    def one_step(k, *done):
        ones[k] = one_cross(wide_x, wide_a[k], PIECES[k][0], *done)

    def two_step(k, *done):
        blocks = (xs[k], ps[k], qs[k], fs[k], bases[k], own[k], others[k], other[k])
        twos[k] = pair_cross(blocks, *done)

    wide_x = exchange(xv)
    send_piece(0)
    send_piece(1)
    for k in (2, 3, 4):
        send_piece(k, xs[1])
    base = base_terms(initial, target, step_size * gen_small[0].T, step_size * gen_large[1], xs[4])
    one_first = one_terms(wide_x, mode_one, 0, half, base, ps[0], qs[0], ps[1], qs[1])
    one_second = one_terms(wide_x, mode_one, half, deep - half, one_first)
    back = [exchange(one_first), exchange(one_second)]
    terms_step(0, one_second)
    terms_step(1, own[0], ps[2], ps[3], ps[4])
    base_step(0, own[1])
    base_step(1, bases[0])
    base_step(2, bases[1])
    base_step(3, bases[2])
    base_step(4, bases[3])
    finish(0, bases[4])
    two_step(0, adjoints[0])
    terms_step(2, twos[0])
    two_step(1, own[2])
    terms_step(3, twos[1])
    finish(1, own[3])
    one_step(0, adjoints[1])
    two_step(2, ones[0])
    terms_step(4, twos[2], far[3], others[3])
    finish(2, own[4])
    one_step(1, adjoints[2])
    finish(3, ones[1])
    two_step(3, adjoints[3])
    one_step(2, twos[3])
    finish(4, ones[2])
    cross_zero, cross_three = local_cross(xv, adjoints)
    one_step(3, cross_three)
    two_step(4, ones[3])
    one_step(4, twos[4])
    cross_one = jnp.sum(jnp.concatenate(ones, axis=0), axis=0)
    found = jnp.where(inner, jnp.sum(jnp.concatenate(twos, axis=0), axis=0), 0.0)
    cross_two = jnp.einsum("xr,xy,yc->rc", spread, found, spread[: 2 * part], precision=highest)

    packed = jnp.concatenate(
        [jnp.concatenate([cross_zero, cross_one], axis=1), cross_two, cross_three], axis=0
    )
    def partner(value, axis, step):
        return lax.ppermute(value, axis, [(i, i ^ step) for i in range(lax.axis_size(axis))])

    for axis, step in (("narrow", 1), ("narrow", 2), ("wide", 1), ("wide", 2)):
        packed = packed + partner(packed, axis, step)
    arrays = (packed, partner(packed, "wide", 4), open_small, open_large)
    grad_small, grad_large = run(
        functools.partial(
            last_body,
            math.sqrt(size_small * size_large * size_large),
            math.sqrt(size_small * size_small * size_large),
        ),
        (1,),
        [whole(array) for array in arrays],
        [whole(open_small), whole(open_large)],
        [jax.ShapeDtypeStruct(open_small.shape, f32), jax.ShapeDtypeStruct(open_large.shape, f32)],
        arrays,
        (),
    )
    return (grad_small, grad_large)


def enter_first(tensor):
    return lax.all_to_all(tensor, "wide", split_axis=0, concat_axis=1, tiled=True)


def leave_first(tensor):
    return lax.all_to_all(tensor, "wide", split_axis=1, concat_axis=0, tiled=True)


def enter_second(tensor):
    return lax.all_to_all(tensor, "narrow", split_axis=0, concat_axis=2, tiled=True)


def leave_second(tensor):
    return lax.all_to_all(tensor, "narrow", split_axis=2, concat_axis=0, tiled=True)


def rearranged(tensor):
    return (enter_first(tensor), enter_second(tensor))


def local_part(tensor, mode_zero, mode_three):
    local_terms = jnp.einsum("abcd,ae->ebcd", tensor, mode_zero, precision=highest)
    return local_terms + jnp.einsum("abcd,de->abce", tensor, mode_three, precision=highest)


def operate(tensor, matrices, weights):
    mode_zero, mode_one, mode_two, mode_three, spare_one, spare_two, rim_one, rim_two = matrices
    weight_part, weight_last, weight_tail = weights
    local_terms = local_part(tensor, mode_zero, mode_three)
    tensor_wide = enter_first(tensor)
    tensor_narrow = enter_second(tensor)
    lifted = tensor_wide * weight_part[:, None, None, None]
    wide_terms = jnp.einsum("abcd,be->aecd", tensor_wide, mode_one, precision=highest)
    wide_terms = (
        wide_terms
        + jnp.einsum("abcd,be->aecd", lifted, spare_one, precision=highest)
        - lifted * rim_one[None, :, None, None]
    )
    lowered = tensor_narrow * weight_last[None, None, None, :]
    narrow_terms = jnp.einsum("abcd,ce->abed", tensor_narrow, mode_two, precision=highest)
    narrow_terms = (
        narrow_terms
        + jnp.einsum("abcd,ce->abed", lowered, spare_two, precision=highest)
        - lowered * rim_two[None, None, :, None]
    )
    return (
        local_terms + leave_first(wide_terms) + leave_second(narrow_terms),
        tensor_wide,
        tensor_narrow,
    )


def cross_terms(state_prev, adjoint_now, state_wide, adjoint_wide, state_narrow, adjoint_narrow):
    cross_zero = jnp.einsum("abcd,ebcd->ae", state_prev, adjoint_now, precision=highest)
    cross_three = jnp.einsum("abcd,abce->de", state_prev, adjoint_now, precision=highest)
    cross_one = jnp.einsum("abcd,aecd->be", state_wide, adjoint_wide, precision=highest)
    cross_two = jnp.einsum("abcd,abed->ce", state_narrow, adjoint_narrow, precision=highest)
    return (jnp.stack([cross_zero, cross_one]), jnp.stack([cross_two, cross_three]))


def on_device(
    initial,
    target,
    rates_small,
    rates_large,
    pattern_small,
    pattern_large,
    spare_small,
    spare_large,
    trigger_first,
    trigger_last,
):
    gen_small, exit_small, open_small = generator(rates_small, pattern_small)
    gen_large, exit_large, open_large = generator(rates_large, pattern_large)
    rim_one = jnp.sum(spare_small, axis=1)
    rim_two = jnp.sum(spare_large, axis=1)
    weight_first = trigger_first.astype(jnp.float32)
    weight_last = trigger_last.astype(jnp.float32)
    bound = jnp.sum(jnp.max(exit_small, axis=1)) + jnp.sum(jnp.max(exit_large, axis=1))
    bound = (
        bound + jnp.max(weight_first) * jnp.max(rim_one) + jnp.max(weight_last) * jnp.max(rim_two)
    )
    step_size = 1.0 / bound
    wide_pos = lax.axis_index("wide")
    rows_wide = initial.shape[0] // lax.axis_size("wide")
    weight_part = lax.dynamic_slice_in_dim(weight_first, wide_pos * rows_wide, rows_wide)
    narrow_pos = lax.axis_index("narrow")
    rows_narrow = initial.shape[3] // lax.axis_size("narrow")
    weight_tail = lax.dynamic_slice_in_dim(weight_last, narrow_pos * rows_narrow, rows_narrow)
    weights = (weight_part, weight_last, weight_tail)
    onward = (
        gen_small[0],
        gen_small[1],
        gen_large[0],
        gen_large[1],
        spare_small,
        spare_large,
        rim_one,
        rim_two,
    )
    new_terms, start_wide, start_narrow = operate(initial, onward, weights)
    state = initial + step_size * new_terms
    adjoint = state - target
    adjoint_wide, adjoint_narrow = rearranged(adjoint)
    again_wide, again_narrow = rearranged(initial)
    terms = cross_terms(initial, adjoint, again_wide, adjoint_wide, again_narrow, adjoint_narrow)
    small, large = lax.psum((terms[0], terms[1]), ("wide", "narrow"))
    size_small = initial.shape[0]
    size_large = initial.shape[3]
    small = small / math.sqrt(size_small * size_large * size_large)
    large = large / math.sqrt(size_small * size_small * size_large)
    grad_small = open_small * (small - jnp.diagonal(small, axis1=1, axis2=2)[:, :, None])
    grad_large = open_large * (large - jnp.diagonal(large, axis1=1, axis2=2)[:, :, None])
    return (grad_small, grad_large)


def solution(mesh):
    line = mesh.shape["narrow"] == 4 and mesh.shape["wide"] == 8
    return jax.shard_map(
        line_device if line else on_device,
        mesh=mesh,
        in_specs=(
            P(None, "wide", "narrow", None),
            P(None, "wide", "narrow", None),
            P(),
            P(),
            P(),
            P(),
            P(),
            P(),
            P(),
            P(),
        ),
        out_specs=(P(), P()),
        check_vma=False,
    )
```

```python
import functools
import math

import jax
import jax.numpy as jnp
from jax import lax
from jax.experimental import pallas as pl
from jax.experimental.pallas import tpu as pltpu
from jax.sharding import PartitionSpec as P

highest = lax.Precision.HIGHEST
f32 = jnp.float32
VMEM_LIMIT = 40 * 1024 * 1024
bf16 = jnp.bfloat16

TO_INNER = [(0, 1), (3, 2)]
INNER_SWAP = [(1, 2), (2, 1)]
TO_OUTER = [(1, 0), (2, 3)]

PIECES = [(0, 2), (2, 4), (4, 6), (6, 7), (7, 8)]

ROWS_BY_ROWS = (((1,), (1,)), ((), ()))
DEPTH_BY_DEPTH = (((0,), (0,)), ((), ()))


def generator(rate_matrix, pattern):
    extent = rate_matrix.shape[-1]
    identity = jnp.eye(extent, dtype=jnp.float32)
    opened = pattern.astype(jnp.float32) * (1.0 - identity)
    flow_rates = rate_matrix * opened
    leaving = jnp.sum(flow_rates, axis=-1)
    return (flow_rates - leaving[..., :, None] * identity, leaving, opened)


def halves(value):
    high = value.astype(bf16)
    low = (value - high.astype(f32)).astype(bf16)
    return high, low


def run(body, grid, in_specs, out_specs, out_shape, args, done):
    count, extra = len(args), len(done)

    def kernel(*refs):
        body(*refs[:count], *refs[count + extra :])

    return pl.pallas_call(
        kernel,
        grid=grid,
        in_specs=list(in_specs) + [pl.BlockSpec(memory_space=pltpu.HBM)] * extra,
        out_specs=out_specs,
        out_shape=out_shape,
        compiler_params=pltpu.CompilerParams(vmem_limit_bytes=VMEM_LIMIT),
        cost_estimate=pl.CostEstimate(flops=0, bytes_accessed=0, transcendentals=0),
    )(*args, *done)


def whole(array):
    return pl.BlockSpec(array.shape, lambda i: (0,) * array.ndim)


def stacked_rows(ref, count, inner, at):
    rows = [ref[pl.ds(at + k, count, stride=inner), :] for k in (0, 1)]
    high, low = halves(jnp.concatenate(rows, axis=1))
    return jnp.concatenate([high, low], axis=0)


def left_parts(matrix):
    high, low = halves(matrix)
    return jnp.concatenate(
        [jnp.concatenate([high, high], axis=1), jnp.concatenate([low, low], axis=1)], axis=0
    )


def folded(total):
    rows, cols = total.shape[0] // 2, total.shape[1] // 2
    total = total[:rows] + total[rows:]
    return total[:, :cols] + total[:, cols:]


def product(matrix, in_ref, out_ref, count, inner, add):
    width = in_ref.shape[1]
    for at in range(0, inner, 2):
        out = jnp.dot(matrix, stacked_rows(in_ref, count, inner, at), preferred_element_type=f32)
        out = out[:count] + out[count:]
        for k in (0, 1):
            place = pl.ds(at + k, count, stride=inner)
            piece = out[:, k * width : (k + 1) * width]
            out_ref[place, :] = out_ref[place, :] + piece if add else piece


def base_body(x_ref, t_ref, first_ref, last_ref, o_ref):
    count, _, inner, width = x_ref.shape
    x2, t2, o2 = (ref.reshape(count * inner, width) for ref in (x_ref, t_ref, o_ref))
    high, low = halves(last_ref[...])
    last = jnp.concatenate([jnp.concatenate([high, low], axis=1)] * 2, axis=0)
    for r in range(0, count * inner, 256):
        x = x2[r : r + 256]
        high, low = halves(x)
        out = jnp.dot(jnp.concatenate([high, low], axis=1), last, preferred_element_type=f32)
        o2[r : r + 256] = x - t2[r : r + 256] + (out[:, :width] + out[:, width:])
    product(left_parts(first_ref[...]), x2, o2, count, inner, True)


def base_terms(x, t, first, last, *done):
    block = pl.BlockSpec((x.shape[0], 1) + x.shape[2:], lambda i: (0, i, 0, 0))
    return run(
        base_body,
        (x.shape[1],),
        [block, block, whole(first), whole(last)],
        block,
        jax.ShapeDtypeStruct(x.shape, f32),
        (x, t, first, last,),
        done,
    )


def one_body(x_ref, k_ref, o_ref):
    blocks, _, rows, inner, width = x_ref.shape
    count = blocks * rows
    x2, o2 = x_ref.reshape(count * inner, width), o_ref.reshape(count * inner, width)
    product(left_parts(k_ref[0]), x2, o2, count, inner, False)


def one_terms(x, matrices, skip, states, *done):
    block = lambda skip: pl.BlockSpec((x.shape[0], 1) + x.shape[2:], lambda i: (0, i + skip, 0, 0, 0))
    return run(
        one_body,
        (states,),
        [block(skip), pl.BlockSpec((1,) + matrices.shape[1:], lambda i: (i + skip, 0, 0))],
        block(0),
        jax.ShapeDtypeStruct((x.shape[0], states) + x.shape[2:], f32),
        (x, matrices,),
        done,
    )


def one_cross_body(x_ref, a_ref, o_ref):
    blocks, _, rows, inner, width = x_ref.shape
    count = blocks * rows
    x2, a2 = x_ref.reshape(count * inner, width), a_ref.reshape(count * inner, width)
    total = None
    for at in range(0, inner, 2):
        term = lax.dot_general(
            stacked_rows(x2, count, inner, at),
            stacked_rows(a2, count, inner, at),
            ROWS_BY_ROWS,
            preferred_element_type=f32,
        )
        total = term if total is None else total + term
    o_ref[0] = folded(total)


def one_cross(x, a, skip, *done):
    count = x.shape[0] * x.shape[2]
    shape = (x.shape[0], 1) + x.shape[2:]
    out = run(
        one_cross_body,
        (a.shape[1],),
        [
            pl.BlockSpec(shape, lambda i: (0, i + skip, 0, 0, 0)),
            pl.BlockSpec(shape, lambda i: (0, i, 0, 0, 0)),
        ],
        pl.BlockSpec((1, count, count), lambda i: (i, 0, 0)),
        jax.ShapeDtypeStruct((a.shape[1], count, count), f32),
        (x, a,),
        done,
    )
    return out


def local_body(pieces, x_ref, *refs):
    a_refs, o_ref, o3_ref = refs[: len(pieces)], refs[-2], refs[-1]
    wide, deep, _, inner, width = x_ref.shape
    x2 = x_ref.reshape(wide * deep * inner, width)
    flat = [a.reshape(a.shape[0] * a.shape[1] * inner, width) for a in a_refs]
    total = None
    for at in range(0, inner, 2):
        parts = []
        for k in (0, 1):
            rows = [
                a[pl.ds(at + k, wide * (hi - lo), stride=inner), :] for a, (lo, hi) in zip(flat, pieces)
            ]
            parts.append(jnp.concatenate(rows, axis=0))
        high, low = halves(jnp.concatenate(parts, axis=1))
        term = lax.dot_general(
            stacked_rows(x2, wide * deep, inner, at),
            jnp.concatenate([high, low], axis=0),
            ROWS_BY_ROWS,
            preferred_element_type=f32,
        )
        total = term if total is None else total + term
    o_ref[0] = folded(total)
    total = None
    for a_ref, (lo, hi) in zip(a_refs, pieces):
        for s in range(lo, hi):
            sides = []
            for ref, at in ((x_ref, s), (a_ref, s - lo)):
                rows = jnp.concatenate([ref[w, at, 0] for w in range(wide)], axis=0)
                sides.append(jnp.concatenate(halves(rows), axis=1))
            term = lax.dot_general(sides[0], sides[1], DEPTH_BY_DEPTH, preferred_element_type=f32)
            total = term if total is None else total + term
    o3_ref[0] = folded(total)


def local_cross(x, adjoints, *done):
    wide, deep, rows, inner, width = x.shape
    block = lambda a: pl.BlockSpec((wide, a.shape[1], 1, inner, width), lambda i: (0, 0, i, 0, 0))
    count = wide * deep
    zero, three = run(
        functools.partial(local_body, PIECES),
        (rows,),
        [block(x)] + [block(a) for a in adjoints],
        [
            pl.BlockSpec((1, count, count), lambda i: (i, 0, 0)),
            pl.BlockSpec((1, width, width), lambda i: (i, 0, 0)),
        ],
        [
            jax.ShapeDtypeStruct((rows, count, count), f32),
            jax.ShapeDtypeStruct((rows, width, width), f32),
        ],
        (x, *adjoints,),
        done,
    )
    zero = jnp.sum(zero, axis=0)
    columns, at = [], 0
    for lo, hi in PIECES:
        size = wide * (hi - lo)
        columns.append(zero[:, at : at + size].reshape(count, wide, hi - lo))
        at += size
    zero = jnp.concatenate(columns, axis=2).reshape(count, count)
    return zero, jnp.sum(three, axis=0)


def block_pair(refs, n):
    sides = [jnp.concatenate([ref[k] for ref in refs], axis=0) for k in (n, n + 1)]
    high, low = halves(jnp.concatenate(sides, axis=1))
    return jnp.concatenate([high, low], axis=0)


def pair_terms_body(w_ref, m_ref, x_ref, p_ref, q_ref, f_ref, own_ref, other_ref):
    cells, part, width = x_ref.shape
    weights = left_parts(m_ref[...])
    gate = jnp.concatenate([w_ref[...], w_ref[...]], axis=1)
    for n in range(0, cells, 2):
        both = block_pair((x_ref, p_ref, q_ref, f_ref), n)
        out = jnp.dot(weights, both, preferred_element_type=f32)
        rows = out.shape[0] // 2
        out = out[:rows] + out[rows:]
        out = out[: rows // 2] + gate * out[rows // 2 :]
        for k in (0, 1):
            own_ref[n + k] = out[:part, k * width : (k + 1) * width]
            other_ref[n + k] = out[part:, k * width : (k + 1) * width]


def pair_cross_body(x_ref, p_ref, q_ref, f_ref, own_ref, base_ref, terms_ref, c_ref):
    total = None
    for n in range(0, x_ref.shape[0], 2):
        sides = [
            jnp.concatenate([own_ref[k], base_ref[k] + terms_ref[k]], axis=0) for k in (n, n + 1)
        ]
        high, low = halves(jnp.concatenate(sides, axis=1))
        term = lax.dot_general(
            block_pair((x_ref, p_ref, q_ref, f_ref), n),
            jnp.concatenate([high, low], axis=0),
            ROWS_BY_ROWS,
            preferred_element_type=f32,
        )
        total = term if total is None else total + term
    c_ref[0] = folded(total)


def pair_terms(gate, weights, blocks, *done):
    count, part, width = blocks[0].shape
    cells = 16
    block = pl.BlockSpec((cells, part, width), lambda i: (i, 0, 0))
    return run(
        pair_terms_body,
        (count // cells,),
        [whole(gate), whole(weights)] + [block] * 4,
        [block, block],
        [jax.ShapeDtypeStruct(blocks[0].shape, f32)] * 2,
        (gate, weights, *blocks,),
        done,
    )


def pair_cross(blocks, *done):
    count, part, width = blocks[0].shape
    cells = 16
    block = pl.BlockSpec((cells, part, width), lambda i: (i, 0, 0))
    shape = (count // cells, 4 * part, 2 * part)
    return run(
        pair_cross_body,
        (count // cells,),
        [block] * 7,
        pl.BlockSpec((1,) + shape[1:], lambda i: (i, 0, 0)),
        jax.ShapeDtypeStruct(shape, f32),
        (*blocks,),
        done,
    )


def last_body(scale_small, scale_large, a_ref, b_ref, small_ref, large_ref, s_ref, l_ref):
    total = a_ref[...] + b_ref[...]

    def gradient(cross, opened):
        same = lax.broadcasted_iota(jnp.int32, cross.shape, 0) == lax.broadcasted_iota(jnp.int32, cross.shape, 1)
        diagonal = jnp.sum(jnp.where(same, cross, 0.0), axis=1, keepdims=True)
        return opened * (cross - diagonal)

    small, large = s_ref.shape[1], l_ref.shape[1]
    for k in (0, 1):
        cross = total[:small, k * small : (k + 1) * small] / scale_small
        s_ref[k] = gradient(cross, small_ref[k])
        cross = total[small + k * large : small + (k + 1) * large] / scale_large
        l_ref[k] = gradient(cross, large_ref[k])


def copy_body(x_ref, o_ref):
    o_ref[...] = x_ref[...]


def sum_body(*refs):
    total = refs[0][...]
    for ref in refs[1:-1]:
        total = total + ref[...]
    refs[-1][...] = total


def piece_of(lo, hi, skip, shape):
    size = hi - lo
    return pl.BlockSpec((1, size) + shape[2:], lambda i: (i, (lo - skip) // size, 0, 0, 0))


def cut_piece(x, lo, hi, *done):
    out = jax.ShapeDtypeStruct((x.shape[0], hi - lo) + x.shape[2:], f32)
    return run(
        copy_body, (x.shape[0],), [piece_of(lo, hi, 0, x.shape)], piece_of(lo, hi, lo, x.shape), out, (x,), done
    )


def add_piece(x, y, skip, lo, hi, *done):
    out = jax.ShapeDtypeStruct((x.shape[0], hi - lo) + x.shape[2:], f32)
    return run(
        sum_body,
        (x.shape[0],),
        [piece_of(lo, hi, 0, x.shape), piece_of(lo, hi, skip, x.shape)],
        piece_of(lo, hi, lo, x.shape),
        out,
        (x, y),
        done,
    )


def add_all(arrays, *done):
    shape = arrays[0].shape
    block = pl.BlockSpec((shape[0] // 4,) + shape[1:], lambda i: (i, 0, 0))
    out = jax.ShapeDtypeStruct(shape, f32)
    return run(sum_body, (4,), [block] * len(arrays), block, out, tuple(arrays), done)


def line_device(
    initial, target, rates_small, rates_large, pattern_small, pattern_large,
    spare_small, spare_large, trigger_first, trigger_last,
):
    gen_small, exit_small, open_small = generator(rates_small, pattern_small)
    gen_large, exit_large, open_large = generator(rates_large, pattern_large)
    rim_one = jnp.sum(spare_small, axis=1)
    rim_two = jnp.sum(spare_large, axis=1)
    weight_first = trigger_first.astype(f32)
    weight_last = trigger_last.astype(f32)
    bound = jnp.sum(jnp.max(exit_small, axis=1)) + jnp.sum(jnp.max(exit_large, axis=1))
    bound = bound + jnp.max(weight_first) * jnp.max(rim_one) + jnp.max(weight_last) * jnp.max(rim_two)
    step_size = 1.0 / bound

    size_small, size_large = initial.shape[0], initial.shape[3]
    wide = lax.axis_size("wide")
    wide_pos = lax.axis_index("wide")
    place = lax.axis_index("narrow")
    deep = size_small // wide
    rows, part = initial.shape[1], initial.shape[2]

    spare_one = spare_small - jnp.diag(rim_one)
    mine = lax.dynamic_slice_in_dim(weight_first, wide_pos * deep, deep)
    mode_one = step_size * (gen_small[1][None] + mine[:, None, None] * spare_one[None])
    mode_one = mode_one.transpose(0, 2, 1)

    inner = (place == 1) | (place == 2)
    partner = jnp.where(place < 2, 1 - place, 5 - place)
    spare_two = spare_large - jnp.diag(rim_two)
    factor = jnp.where(inner, step_size, 0.0)
    places = jnp.concatenate(
        [jnp.arange(part) + block * part for block in (place, partner, 3 - place, 3 - partner)]
    )
    spread = (places[:, None] == jnp.arange(size_large)[None]).astype(f32)
    picked = functools.partial(jnp.einsum, "xr,rc,yc->xy", precision=highest)
    weights = factor * jnp.concatenate(
        [picked(spread, m, spread[: 2 * part]) for m in (gen_large[0], spare_two)], axis=1
    ).T
    gate = weight_last[None, :]

    xv = initial.reshape(wide, deep, rows, part, size_large)
    half = deep // 2

    def shift(value, pairs):
        return lax.ppermute(value, "narrow", pairs)

    def exchange(value):
        return lax.all_to_all(value, "wide", 0, 0, tiled=True)

    count = len(PIECES)
    xs, ps, qs, fs = ([None] * count for _ in range(4))
    bases, others, own, other, far = ([None] * count for _ in range(5))
    adjoints, wide_a, ones, twos = ([None] * count for _ in range(4))

    def flat(value):
        return value.reshape(-1, part, size_large)

    def send_piece(k, *done):
        xs[k] = flat(cut_piece(xv, *PIECES[k], *done))
        ps[k] = shift(xs[k], TO_INNER)
        qs[k] = shift(xs[k], INNER_SWAP)
        fs[k] = shift(ps[k], INNER_SWAP)

    def base_step(k, *done):
        lo, hi = PIECES[k]
        bases[k] = flat(add_piece(base.reshape(xv.shape), back[lo // half], lo // half * half, lo, hi, *done))
        others[k] = shift(bases[k], TO_INNER)

    def terms_step(k, *done):
        own[k], other[k] = pair_terms(gate, weights, (xs[k], ps[k], qs[k], fs[k]), *done)
        far[k] = shift(other[k], TO_OUTER)

    def finish(k, *done):
        lo, hi = PIECES[k]
        total = add_all((own[k], far[k], bases[k]), *done)
        adjoints[k] = total.reshape(wide, hi - lo, rows, part, size_large)
        wide_a[k] = exchange(adjoints[k])

    def one_step(k, *done):
        ones[k] = one_cross(wide_x, wide_a[k], PIECES[k][0], *done)

    def two_step(k, *done):
        twos[k] = pair_cross((xs[k], ps[k], qs[k], fs[k], flat(adjoints[k]), others[k], other[k]), *done)

    wide_x = exchange(xv)
    send_piece(0)
    send_piece(1)
    for k in (2, 3, 4):
        send_piece(k, xs[1])
    base = base_terms(initial, target, step_size * gen_small[0].T, step_size * gen_large[1], xs[4])
    one_first = one_terms(wide_x, mode_one, 0, half, base, ps[0], qs[0], ps[1], qs[1])
    one_second = one_terms(wide_x, mode_one, half, deep - half, one_first)
    back = [exchange(one_first), exchange(one_second)]
    terms_step(0, one_second)
    base_step(0, own[0])
    base_step(1, bases[0])
    terms_step(1, bases[1], ps[2], ps[3], ps[4])
    base_step(2, own[1])
    base_step(3, bases[2])
    base_step(4, bases[3])
    finish(0, bases[4])
    terms_step(2, adjoints[0])
    finish(1, own[2])
    two_step(0, adjoints[1])
    two_step(1, twos[0])
    terms_step(3, twos[1])
    finish(2, own[3])
    one_step(0, adjoints[2])
    one_step(1, ones[0])
    two_step(2, ones[1])
    terms_step(4, twos[2])
    finish(3, own[4])
    one_step(2, adjoints[3])
    two_step(3, ones[2])
    finish(4, twos[3])
    cross_zero, cross_three = local_cross(xv, adjoints)
    two_step(4, cross_three)
    one_step(3, twos[4])
    one_step(4, ones[3])
    cross_one = jnp.sum(jnp.concatenate(ones, axis=0), axis=0)
    found = jnp.where(inner, jnp.sum(jnp.concatenate(twos, axis=0), axis=0), 0.0)
    cross_two = jnp.einsum("xr,xy,yc->rc", spread, found, spread[: 2 * part], precision=highest)

    packed = jnp.concatenate(
        [jnp.concatenate([cross_zero, cross_one], axis=1), cross_two, cross_three], axis=0
    )
    def partner(value, axis, step):
        return lax.ppermute(value, axis, [(i, i ^ step) for i in range(lax.axis_size(axis))])

    for axis, step in (("wide", 1), ("wide", 2), ("wide", 4), ("narrow", 1)):
        packed = packed + partner(packed, axis, step)
    arrays = (packed, partner(packed, "narrow", 2), open_small, open_large)
    grad_small, grad_large = run(
        functools.partial(
            last_body,
            math.sqrt(size_small * size_large * size_large),
            math.sqrt(size_small * size_small * size_large),
        ),
        (1,),
        [whole(array) for array in arrays],
        [whole(open_small), whole(open_large)],
        [jax.ShapeDtypeStruct(open_small.shape, f32), jax.ShapeDtypeStruct(open_large.shape, f32)],
        arrays,
        (),
    )
    return (grad_small, grad_large)


def enter_first(tensor):
    return lax.all_to_all(tensor, "wide", split_axis=0, concat_axis=1, tiled=True)


def leave_first(tensor):
    return lax.all_to_all(tensor, "wide", split_axis=1, concat_axis=0, tiled=True)


def enter_second(tensor):
    return lax.all_to_all(tensor, "narrow", split_axis=0, concat_axis=2, tiled=True)


def leave_second(tensor):
    return lax.all_to_all(tensor, "narrow", split_axis=2, concat_axis=0, tiled=True)


def rearranged(tensor):
    return (enter_first(tensor), enter_second(tensor))


def local_part(tensor, mode_zero, mode_three):
    local_terms = jnp.einsum("abcd,ae->ebcd", tensor, mode_zero, precision=highest)
    return local_terms + jnp.einsum("abcd,de->abce", tensor, mode_three, precision=highest)


def operate(tensor, matrices, weights):
    mode_zero, mode_one, mode_two, mode_three, spare_one, spare_two, rim_one, rim_two = matrices
    weight_part, weight_last, weight_tail = weights
    local_terms = local_part(tensor, mode_zero, mode_three)
    tensor_wide = enter_first(tensor)
    tensor_narrow = enter_second(tensor)
    lifted = tensor_wide * weight_part[:, None, None, None]
    wide_terms = jnp.einsum("abcd,be->aecd", tensor_wide, mode_one, precision=highest)
    wide_terms = (
        wide_terms
        + jnp.einsum("abcd,be->aecd", lifted, spare_one, precision=highest)
        - lifted * rim_one[None, :, None, None]
    )
    lowered = tensor_narrow * weight_last[None, None, None, :]
    narrow_terms = jnp.einsum("abcd,ce->abed", tensor_narrow, mode_two, precision=highest)
    narrow_terms = (
        narrow_terms
        + jnp.einsum("abcd,ce->abed", lowered, spare_two, precision=highest)
        - lowered * rim_two[None, None, :, None]
    )
    return (
        local_terms + leave_first(wide_terms) + leave_second(narrow_terms),
        tensor_wide,
        tensor_narrow,
    )


def cross_terms(state_prev, adjoint_now, state_wide, adjoint_wide, state_narrow, adjoint_narrow):
    cross_zero = jnp.einsum("abcd,ebcd->ae", state_prev, adjoint_now, precision=highest)
    cross_three = jnp.einsum("abcd,abce->de", state_prev, adjoint_now, precision=highest)
    cross_one = jnp.einsum("abcd,aecd->be", state_wide, adjoint_wide, precision=highest)
    cross_two = jnp.einsum("abcd,abed->ce", state_narrow, adjoint_narrow, precision=highest)
    return (jnp.stack([cross_zero, cross_one]), jnp.stack([cross_two, cross_three]))


def on_device(
    initial,
    target,
    rates_small,
    rates_large,
    pattern_small,
    pattern_large,
    spare_small,
    spare_large,
    trigger_first,
    trigger_last,
):
    gen_small, exit_small, open_small = generator(rates_small, pattern_small)
    gen_large, exit_large, open_large = generator(rates_large, pattern_large)
    rim_one = jnp.sum(spare_small, axis=1)
    rim_two = jnp.sum(spare_large, axis=1)
    weight_first = trigger_first.astype(jnp.float32)
    weight_last = trigger_last.astype(jnp.float32)
    bound = jnp.sum(jnp.max(exit_small, axis=1)) + jnp.sum(jnp.max(exit_large, axis=1))
    bound = (
        bound + jnp.max(weight_first) * jnp.max(rim_one) + jnp.max(weight_last) * jnp.max(rim_two)
    )
    step_size = 1.0 / bound
    wide_pos = lax.axis_index("wide")
    rows_wide = initial.shape[0] // lax.axis_size("wide")
    weight_part = lax.dynamic_slice_in_dim(weight_first, wide_pos * rows_wide, rows_wide)
    narrow_pos = lax.axis_index("narrow")
    rows_narrow = initial.shape[3] // lax.axis_size("narrow")
    weight_tail = lax.dynamic_slice_in_dim(weight_last, narrow_pos * rows_narrow, rows_narrow)
    weights = (weight_part, weight_last, weight_tail)
    onward = (
        gen_small[0],
        gen_small[1],
        gen_large[0],
        gen_large[1],
        spare_small,
        spare_large,
        rim_one,
        rim_two,
    )
    new_terms, start_wide, start_narrow = operate(initial, onward, weights)
    state = initial + step_size * new_terms
    adjoint = state - target
    adjoint_wide, adjoint_narrow = rearranged(adjoint)
    again_wide, again_narrow = rearranged(initial)
    terms = cross_terms(initial, adjoint, again_wide, adjoint_wide, again_narrow, adjoint_narrow)
    small, large = lax.psum((terms[0], terms[1]), ("wide", "narrow"))
    size_small = initial.shape[0]
    size_large = initial.shape[3]
    small = small / math.sqrt(size_small * size_large * size_large)
    large = large / math.sqrt(size_small * size_small * size_large)
    grad_small = open_small * (small - jnp.diagonal(small, axis1=1, axis2=2)[:, :, None])
    grad_large = open_large * (large - jnp.diagonal(large, axis1=1, axis2=2)[:, :, None])
    return (grad_small, grad_large)


def solution(mesh):
    line = mesh.shape["narrow"] == 4 and mesh.shape["wide"] == 8
    return jax.shard_map(
        line_device if line else on_device,
        mesh=mesh,
        in_specs=(
            P(None, "wide", "narrow", None),
            P(None, "wide", "narrow", None),
            P(),
            P(),
            P(),
            P(),
            P(),
            P(),
            P(),
            P(),
        ),
        out_specs=(P(), P()),
        check_vma=False,
    )
```

```python
import functools
import math

import jax
import jax.numpy as jnp
from jax import lax
from jax.experimental import pallas as pl
from jax.experimental.pallas import tpu as pltpu
from jax.sharding import PartitionSpec as P

highest = lax.Precision.HIGHEST
f32 = jnp.float32
VMEM_LIMIT = 40 * 1024 * 1024
bf16 = jnp.bfloat16

TO_INNER = [(0, 1), (3, 2)]
INNER_SWAP = [(1, 2), (2, 1)]
TO_OUTER = [(1, 0), (2, 3)]

PIECES = [(0, 2), (2, 4), (4, 6), (6, 7), (7, 8)]

ROWS_BY_ROWS = (((1,), (1,)), ((), ()))
DEPTH_BY_DEPTH = (((0,), (0,)), ((), ()))


def generator(rate_matrix, pattern):
    extent = rate_matrix.shape[-1]
    identity = jnp.eye(extent, dtype=jnp.float32)
    opened = pattern.astype(jnp.float32) * (1.0 - identity)
    flow_rates = rate_matrix * opened
    leaving = jnp.sum(flow_rates, axis=-1)
    return (flow_rates - leaving[..., :, None] * identity, leaving, opened)


def halves(value):
    high = value.astype(bf16)
    low = (value - high.astype(f32)).astype(bf16)
    return high, low


def run(body, grid, in_specs, out_specs, out_shape, args, done, limit=VMEM_LIMIT):
    count, extra = len(args), len(done)

    def kernel(*refs):
        body(*refs[:count], *refs[count + extra :])

    return pl.pallas_call(
        kernel,
        grid=grid,
        in_specs=list(in_specs) + [pl.BlockSpec(memory_space=pltpu.HBM)] * extra,
        out_specs=out_specs,
        out_shape=out_shape,
        compiler_params=pltpu.CompilerParams(vmem_limit_bytes=limit),
        cost_estimate=pl.CostEstimate(flops=0, bytes_accessed=0, transcendentals=0),
    )(*args, *done)


def whole(array):
    return pl.BlockSpec(array.shape, lambda i: (0,) * array.ndim)


def stacked_rows(ref, count, inner, at):
    rows = [ref[pl.ds(at + k, count, stride=inner), :] for k in (0, 1)]
    high, low = halves(jnp.concatenate(rows, axis=1))
    return jnp.concatenate([high, low], axis=0)


def left_parts(matrix):
    high, low = halves(matrix)
    return jnp.concatenate(
        [jnp.concatenate([high, high], axis=1), jnp.concatenate([low, low], axis=1)], axis=0
    )


def folded(total):
    rows, cols = total.shape[0] // 2, total.shape[1] // 2
    total = total[:rows] + total[rows:]
    return total[:, :cols] + total[:, cols:]


def product(matrix, in_ref, out_ref, count, inner, add):
    width = in_ref.shape[1]
    for at in range(0, inner, 2):
        out = jnp.dot(matrix, stacked_rows(in_ref, count, inner, at), preferred_element_type=f32)
        out = out[:count] + out[count:]
        for k in (0, 1):
            place = pl.ds(at + k, count, stride=inner)
            piece = out[:, k * width : (k + 1) * width]
            out_ref[place, :] = out_ref[place, :] + piece if add else piece


def base_body(x_ref, t_ref, first_ref, last_ref, o_ref):
    count, _, inner, width = x_ref.shape
    x2, t2, o2 = (ref.reshape(count * inner, width) for ref in (x_ref, t_ref, o_ref))
    high, low = halves(last_ref[...])
    last = jnp.concatenate([jnp.concatenate([high, low], axis=1)] * 2, axis=0)
    for r in range(0, count * inner, 256):
        x = x2[r : r + 256]
        high, low = halves(x)
        out = jnp.dot(jnp.concatenate([high, low], axis=1), last, preferred_element_type=f32)
        o2[r : r + 256] = x - t2[r : r + 256] + (out[:, :width] + out[:, width:])
    product(left_parts(first_ref[...]), x2, o2, count, inner, True)


def base_terms(x, t, first, last, *done):
    block = pl.BlockSpec((x.shape[0], 1) + x.shape[2:], lambda i: (0, i, 0, 0))
    return run(
        base_body,
        (x.shape[1],),
        [block, block, whole(first), whole(last)],
        block,
        jax.ShapeDtypeStruct(x.shape, f32),
        (x, t, first, last,),
        done,
    )


def one_body(x_ref, k_ref, o_ref):
    blocks, _, rows, inner, width = x_ref.shape
    count = blocks * rows
    x2, o2 = x_ref.reshape(count * inner, width), o_ref.reshape(count * inner, width)
    product(left_parts(k_ref[0]), x2, o2, count, inner, False)


def one_terms(x, matrices, skip, states, *done):
    block = lambda skip: pl.BlockSpec((x.shape[0], 1) + x.shape[2:], lambda i: (0, i + skip, 0, 0, 0))
    return run(
        one_body,
        (states,),
        [block(skip), pl.BlockSpec((1,) + matrices.shape[1:], lambda i: (i + skip, 0, 0))],
        block(0),
        jax.ShapeDtypeStruct((x.shape[0], states) + x.shape[2:], f32),
        (x, matrices,),
        done,
    )


def one_cross_body(x_ref, a_ref, o_ref):
    blocks, _, rows, inner, width = x_ref.shape
    count = blocks * rows
    x2, a2 = x_ref.reshape(count * inner, width), a_ref.reshape(count * inner, width)
    total = None
    for at in range(0, inner, 2):
        term = lax.dot_general(
            stacked_rows(x2, count, inner, at),
            stacked_rows(a2, count, inner, at),
            ROWS_BY_ROWS,
            preferred_element_type=f32,
        )
        total = term if total is None else total + term
    o_ref[0] = folded(total)


def one_cross(x, a, skip, *done):
    count = x.shape[0] * x.shape[2]
    shape = (x.shape[0], 1) + x.shape[2:]
    out = run(
        one_cross_body,
        (a.shape[1],),
        [
            pl.BlockSpec(shape, lambda i: (0, i + skip, 0, 0, 0)),
            pl.BlockSpec(shape, lambda i: (0, i, 0, 0, 0)),
        ],
        pl.BlockSpec((1, count, count), lambda i: (i, 0, 0)),
        jax.ShapeDtypeStruct((a.shape[1], count, count), f32),
        (x, a,),
        done,
    )
    return out


def local_body(pieces, x_ref, *refs):
    a_refs, o_ref, o3_ref = refs[: len(pieces)], refs[-2], refs[-1]
    wide, deep, _, inner, width = x_ref.shape
    x2 = x_ref.reshape(wide * deep * inner, width)
    flat = [a.reshape(a.shape[0] * a.shape[1] * inner, width) for a in a_refs]
    total = None
    for at in range(0, inner, 2):
        parts = []
        for k in (0, 1):
            rows = [
                a[pl.ds(at + k, wide * (hi - lo), stride=inner), :] for a, (lo, hi) in zip(flat, pieces)
            ]
            parts.append(jnp.concatenate(rows, axis=0))
        high, low = halves(jnp.concatenate(parts, axis=1))
        term = lax.dot_general(
            stacked_rows(x2, wide * deep, inner, at),
            jnp.concatenate([high, low], axis=0),
            ROWS_BY_ROWS,
            preferred_element_type=f32,
        )
        total = term if total is None else total + term
    o_ref[0] = folded(total)
    total = None
    for a_ref, (lo, hi) in zip(a_refs, pieces):
        for s in range(lo, hi):
            sides = []
            for ref, at in ((x_ref, s), (a_ref, s - lo)):
                rows = jnp.concatenate([ref[w, at, 0] for w in range(wide)], axis=0)
                sides.append(jnp.concatenate(halves(rows), axis=1))
            term = lax.dot_general(sides[0], sides[1], DEPTH_BY_DEPTH, preferred_element_type=f32)
            total = term if total is None else total + term
    o3_ref[0] = folded(total)


def local_cross(x, adjoints, *done):
    wide, deep, rows, inner, width = x.shape
    block = lambda a: pl.BlockSpec((wide, a.shape[1], 1, inner, width), lambda i: (0, 0, i, 0, 0))
    count = wide * deep
    zero, three = run(
        functools.partial(local_body, PIECES),
        (rows,),
        [block(x)] + [block(a) for a in adjoints],
        [
            pl.BlockSpec((1, count, count), lambda i: (i, 0, 0)),
            pl.BlockSpec((1, width, width), lambda i: (i, 0, 0)),
        ],
        [
            jax.ShapeDtypeStruct((rows, count, count), f32),
            jax.ShapeDtypeStruct((rows, width, width), f32),
        ],
        (x, *adjoints,),
        done,
        56 * 1024 * 1024,
    )
    zero = jnp.sum(zero, axis=0)
    columns, at = [], 0
    for lo, hi in PIECES:
        size = wide * (hi - lo)
        columns.append(zero[:, at : at + size].reshape(count, wide, hi - lo))
        at += size
    zero = jnp.concatenate(columns, axis=2).reshape(count, count)
    return zero, jnp.sum(three, axis=0)


def block_pair(refs, n):
    sides = [jnp.concatenate([ref[k] for ref in refs], axis=0) for k in (n, n + 1)]
    high, low = halves(jnp.concatenate(sides, axis=1))
    return jnp.concatenate([high, low], axis=0)


def pair_terms_body(w_ref, m_ref, x_ref, p_ref, q_ref, f_ref, own_ref, other_ref):
    cells, part, width = x_ref.shape
    weights = left_parts(m_ref[...])
    gate = jnp.concatenate([w_ref[...], w_ref[...]], axis=1)
    for n in range(0, cells, 2):
        both = block_pair((x_ref, p_ref, q_ref, f_ref), n)
        out = jnp.dot(weights, both, preferred_element_type=f32)
        rows = out.shape[0] // 2
        out = out[:rows] + out[rows:]
        out = out[: rows // 2] + gate * out[rows // 2 :]
        for k in (0, 1):
            own_ref[n + k] = out[:part, k * width : (k + 1) * width]
            other_ref[n + k] = out[part:, k * width : (k + 1) * width]


def pair_cross_body(x_ref, p_ref, q_ref, f_ref, own_ref, base_ref, terms_ref, c_ref):
    total = None
    for n in range(0, x_ref.shape[0], 2):
        sides = [
            jnp.concatenate([own_ref[k], base_ref[k] + terms_ref[k]], axis=0) for k in (n, n + 1)
        ]
        high, low = halves(jnp.concatenate(sides, axis=1))
        term = lax.dot_general(
            block_pair((x_ref, p_ref, q_ref, f_ref), n),
            jnp.concatenate([high, low], axis=0),
            ROWS_BY_ROWS,
            preferred_element_type=f32,
        )
        total = term if total is None else total + term
    c_ref[0] = folded(total)


def pair_terms(gate, weights, blocks, *done):
    count, part, width = blocks[0].shape
    cells = 16
    block = pl.BlockSpec((cells, part, width), lambda i: (i, 0, 0))
    return run(
        pair_terms_body,
        (count // cells,),
        [whole(gate), whole(weights)] + [block] * 4,
        [block, block],
        [jax.ShapeDtypeStruct(blocks[0].shape, f32)] * 2,
        (gate, weights, *blocks,),
        done,
    )


def pair_cross(blocks, *done):
    count, part, width = blocks[0].shape
    cells = 16
    block = pl.BlockSpec((cells, part, width), lambda i: (i, 0, 0))
    shape = (count // cells, 4 * part, 2 * part)
    return run(
        pair_cross_body,
        (count // cells,),
        [block] * 7,
        pl.BlockSpec((1,) + shape[1:], lambda i: (i, 0, 0)),
        jax.ShapeDtypeStruct(shape, f32),
        (*blocks,),
        done,
    )


def last_body(scale_small, scale_large, a_ref, b_ref, small_ref, large_ref, s_ref, l_ref):
    total = a_ref[...] + b_ref[...]

    def gradient(cross, opened):
        same = lax.broadcasted_iota(jnp.int32, cross.shape, 0) == lax.broadcasted_iota(jnp.int32, cross.shape, 1)
        diagonal = jnp.sum(jnp.where(same, cross, 0.0), axis=1, keepdims=True)
        return opened * (cross - diagonal)

    small, large = s_ref.shape[1], l_ref.shape[1]
    for k in (0, 1):
        cross = total[:small, k * small : (k + 1) * small] / scale_small
        s_ref[k] = gradient(cross, small_ref[k])
        cross = total[small + k * large : small + (k + 1) * large] / scale_large
        l_ref[k] = gradient(cross, large_ref[k])


def copy_body(x_ref, o_ref):
    o_ref[...] = x_ref[...]


def sum_body(*refs):
    total = refs[0][...]
    for ref in refs[1:-1]:
        total = total + ref[...]
    refs[-1][...] = total


def piece_of(lo, hi, skip, shape):
    size = hi - lo
    return pl.BlockSpec((1, size) + shape[2:], lambda i: (i, (lo - skip) // size, 0, 0, 0))


def cut_piece(x, lo, hi, *done):
    out = jax.ShapeDtypeStruct((x.shape[0], hi - lo) + x.shape[2:], f32)
    return run(
        copy_body, (x.shape[0],), [piece_of(lo, hi, 0, x.shape)], piece_of(lo, hi, lo, x.shape), out, (x,), done
    )


def add_piece(x, y, skip, lo, hi, *done):
    out = jax.ShapeDtypeStruct((x.shape[0], hi - lo) + x.shape[2:], f32)
    return run(
        sum_body,
        (x.shape[0],),
        [piece_of(lo, hi, 0, x.shape), piece_of(lo, hi, skip, x.shape)],
        piece_of(lo, hi, lo, x.shape),
        out,
        (x, y),
        done,
    )


def add_all(arrays, *done):
    shape = arrays[0].shape
    block = pl.BlockSpec((shape[0] // 4,) + shape[1:], lambda i: (i, 0, 0))
    out = jax.ShapeDtypeStruct(shape, f32)
    return run(sum_body, (4,), [block] * len(arrays), block, out, tuple(arrays), done)


def line_device(
    initial, target, rates_small, rates_large, pattern_small, pattern_large,
    spare_small, spare_large, trigger_first, trigger_last,
):
    gen_small, exit_small, open_small = generator(rates_small, pattern_small)
    gen_large, exit_large, open_large = generator(rates_large, pattern_large)
    rim_one = jnp.sum(spare_small, axis=1)
    rim_two = jnp.sum(spare_large, axis=1)
    weight_first = trigger_first.astype(f32)
    weight_last = trigger_last.astype(f32)
    bound = jnp.sum(jnp.max(exit_small, axis=1)) + jnp.sum(jnp.max(exit_large, axis=1))
    bound = bound + jnp.max(weight_first) * jnp.max(rim_one) + jnp.max(weight_last) * jnp.max(rim_two)
    step_size = 1.0 / bound

    size_small, size_large = initial.shape[0], initial.shape[3]
    wide = lax.axis_size("wide")
    wide_pos = lax.axis_index("wide")
    place = lax.axis_index("narrow")
    deep = size_small // wide
    rows, part = initial.shape[1], initial.shape[2]

    spare_one = spare_small - jnp.diag(rim_one)
    mine = lax.dynamic_slice_in_dim(weight_first, wide_pos * deep, deep)
    mode_one = step_size * (gen_small[1][None] + mine[:, None, None] * spare_one[None])
    mode_one = mode_one.transpose(0, 2, 1)

    inner = (place == 1) | (place == 2)
    partner = jnp.where(place < 2, 1 - place, 5 - place)
    spare_two = spare_large - jnp.diag(rim_two)
    factor = jnp.where(inner, step_size, 0.0)
    places = jnp.concatenate(
        [jnp.arange(part) + block * part for block in (place, partner, 3 - place, 3 - partner)]
    )
    spread = (places[:, None] == jnp.arange(size_large)[None]).astype(f32)
    picked = functools.partial(jnp.einsum, "xr,rc,yc->xy", precision=highest)
    weights = factor * jnp.concatenate(
        [picked(spread, m, spread[: 2 * part]) for m in (gen_large[0], spare_two)], axis=1
    ).T
    gate = weight_last[None, :]

    xv = initial.reshape(wide, deep, rows, part, size_large)
    half = deep // 2

    def shift(value, pairs):
        return lax.ppermute(value, "narrow", pairs)

    def exchange(value):
        return lax.all_to_all(value, "wide", 0, 0, tiled=True)

    count = len(PIECES)
    xs, ps, qs, fs = ([None] * count for _ in range(4))
    bases, others, own, other, far = ([None] * count for _ in range(5))
    adjoints, wide_a, ones, twos = ([None] * count for _ in range(4))

    def flat(value):
        return value.reshape(-1, part, size_large)

    def send_piece(k, *done):
        xs[k] = flat(cut_piece(xv, *PIECES[k], *done))
        ps[k] = shift(xs[k], TO_INNER)
        qs[k] = shift(xs[k], INNER_SWAP)
        fs[k] = shift(ps[k], INNER_SWAP)

    def base_step(k, *done):
        lo, hi = PIECES[k]
        bases[k] = flat(add_piece(base.reshape(xv.shape), back[lo // half], lo // half * half, lo, hi, *done))
        others[k] = shift(bases[k], TO_INNER)

    def terms_step(k, *done):
        own[k], other[k] = pair_terms(gate, weights, (xs[k], ps[k], qs[k], fs[k]), *done)
        far[k] = shift(other[k], TO_OUTER)

    def finish(k, *done):
        lo, hi = PIECES[k]
        total = add_all((own[k], far[k], bases[k]), *done)
        adjoints[k] = total.reshape(wide, hi - lo, rows, part, size_large)
        wide_a[k] = exchange(adjoints[k])

    def one_step(k, *done):
        ones[k] = one_cross(wide_x, wide_a[k], PIECES[k][0], *done)

    def two_step(k, *done):
        twos[k] = pair_cross((xs[k], ps[k], qs[k], fs[k], flat(adjoints[k]), others[k], other[k]), *done)

    wide_x = exchange(xv)
    send_piece(0)
    send_piece(1)
    for k in (2, 3, 4):
        send_piece(k, xs[1])
    base = base_terms(initial, target, step_size * gen_small[0].T, step_size * gen_large[1], xs[4])
    one_first = one_terms(wide_x, mode_one, 0, half, base, ps[0], qs[0], ps[1], qs[1])
    one_second = one_terms(wide_x, mode_one, half, deep - half, one_first)
    back = [exchange(one_first), exchange(one_second)]
    terms_step(0, one_second)
    base_step(0, own[0])
    base_step(1, bases[0])
    terms_step(1, bases[1], ps[2], ps[3], ps[4])
    base_step(2, own[1])
    base_step(3, bases[2])
    base_step(4, bases[3])
    finish(0, bases[4])
    terms_step(2, adjoints[0])
    finish(1, own[2])
    two_step(0, adjoints[1])
    two_step(1, twos[0])
    terms_step(3, twos[1])
    finish(2, own[3])
    one_step(0, adjoints[2])
    one_step(1, ones[0])
    two_step(2, ones[1])
    terms_step(4, twos[2])
    finish(3, own[4])
    one_step(2, adjoints[3])
    two_step(3, ones[2])
    finish(4, twos[3])
    cross_zero, cross_three = local_cross(xv, adjoints)
    two_step(4, cross_three)
    one_step(3, twos[4])
    one_step(4, ones[3])
    cross_one = jnp.sum(jnp.concatenate(ones, axis=0), axis=0)
    found = jnp.where(inner, jnp.sum(jnp.concatenate(twos, axis=0), axis=0), 0.0)
    cross_two = jnp.einsum("xr,xy,yc->rc", spread, found, spread[: 2 * part], precision=highest)

    packed = jnp.concatenate(
        [jnp.concatenate([cross_zero, cross_one], axis=1), cross_two, cross_three], axis=0
    )
    def partner(value, axis, step):
        return lax.ppermute(value, axis, [(i, i ^ step) for i in range(lax.axis_size(axis))])

    for axis, step in (("wide", 1), ("wide", 2), ("wide", 4), ("narrow", 1)):
        packed = packed + partner(packed, axis, step)
    arrays = (packed, partner(packed, "narrow", 2), open_small, open_large)
    grad_small, grad_large = run(
        functools.partial(
            last_body,
            math.sqrt(size_small * size_large * size_large),
            math.sqrt(size_small * size_small * size_large),
        ),
        (1,),
        [whole(array) for array in arrays],
        [whole(open_small), whole(open_large)],
        [jax.ShapeDtypeStruct(open_small.shape, f32), jax.ShapeDtypeStruct(open_large.shape, f32)],
        arrays,
        (),
    )
    return (grad_small, grad_large)


def enter_first(tensor):
    return lax.all_to_all(tensor, "wide", split_axis=0, concat_axis=1, tiled=True)


def leave_first(tensor):
    return lax.all_to_all(tensor, "wide", split_axis=1, concat_axis=0, tiled=True)


def enter_second(tensor):
    return lax.all_to_all(tensor, "narrow", split_axis=0, concat_axis=2, tiled=True)


def leave_second(tensor):
    return lax.all_to_all(tensor, "narrow", split_axis=2, concat_axis=0, tiled=True)


def rearranged(tensor):
    return (enter_first(tensor), enter_second(tensor))


def local_part(tensor, mode_zero, mode_three):
    local_terms = jnp.einsum("abcd,ae->ebcd", tensor, mode_zero, precision=highest)
    return local_terms + jnp.einsum("abcd,de->abce", tensor, mode_three, precision=highest)


def operate(tensor, matrices, weights):
    mode_zero, mode_one, mode_two, mode_three, spare_one, spare_two, rim_one, rim_two = matrices
    weight_part, weight_last, weight_tail = weights
    local_terms = local_part(tensor, mode_zero, mode_three)
    tensor_wide = enter_first(tensor)
    tensor_narrow = enter_second(tensor)
    lifted = tensor_wide * weight_part[:, None, None, None]
    wide_terms = jnp.einsum("abcd,be->aecd", tensor_wide, mode_one, precision=highest)
    wide_terms = (
        wide_terms
        + jnp.einsum("abcd,be->aecd", lifted, spare_one, precision=highest)
        - lifted * rim_one[None, :, None, None]
    )
    lowered = tensor_narrow * weight_last[None, None, None, :]
    narrow_terms = jnp.einsum("abcd,ce->abed", tensor_narrow, mode_two, precision=highest)
    narrow_terms = (
        narrow_terms
        + jnp.einsum("abcd,ce->abed", lowered, spare_two, precision=highest)
        - lowered * rim_two[None, None, :, None]
    )
    return (
        local_terms + leave_first(wide_terms) + leave_second(narrow_terms),
        tensor_wide,
        tensor_narrow,
    )


def cross_terms(state_prev, adjoint_now, state_wide, adjoint_wide, state_narrow, adjoint_narrow):
    cross_zero = jnp.einsum("abcd,ebcd->ae", state_prev, adjoint_now, precision=highest)
    cross_three = jnp.einsum("abcd,abce->de", state_prev, adjoint_now, precision=highest)
    cross_one = jnp.einsum("abcd,aecd->be", state_wide, adjoint_wide, precision=highest)
    cross_two = jnp.einsum("abcd,abed->ce", state_narrow, adjoint_narrow, precision=highest)
    return (jnp.stack([cross_zero, cross_one]), jnp.stack([cross_two, cross_three]))


def on_device(
    initial,
    target,
    rates_small,
    rates_large,
    pattern_small,
    pattern_large,
    spare_small,
    spare_large,
    trigger_first,
    trigger_last,
):
    gen_small, exit_small, open_small = generator(rates_small, pattern_small)
    gen_large, exit_large, open_large = generator(rates_large, pattern_large)
    rim_one = jnp.sum(spare_small, axis=1)
    rim_two = jnp.sum(spare_large, axis=1)
    weight_first = trigger_first.astype(jnp.float32)
    weight_last = trigger_last.astype(jnp.float32)
    bound = jnp.sum(jnp.max(exit_small, axis=1)) + jnp.sum(jnp.max(exit_large, axis=1))
    bound = (
        bound + jnp.max(weight_first) * jnp.max(rim_one) + jnp.max(weight_last) * jnp.max(rim_two)
    )
    step_size = 1.0 / bound
    wide_pos = lax.axis_index("wide")
    rows_wide = initial.shape[0] // lax.axis_size("wide")
    weight_part = lax.dynamic_slice_in_dim(weight_first, wide_pos * rows_wide, rows_wide)
    narrow_pos = lax.axis_index("narrow")
    rows_narrow = initial.shape[3] // lax.axis_size("narrow")
    weight_tail = lax.dynamic_slice_in_dim(weight_last, narrow_pos * rows_narrow, rows_narrow)
    weights = (weight_part, weight_last, weight_tail)
    onward = (
        gen_small[0],
        gen_small[1],
        gen_large[0],
        gen_large[1],
        spare_small,
        spare_large,
        rim_one,
        rim_two,
    )
    new_terms, start_wide, start_narrow = operate(initial, onward, weights)
    state = initial + step_size * new_terms
    adjoint = state - target
    adjoint_wide, adjoint_narrow = rearranged(adjoint)
    again_wide, again_narrow = rearranged(initial)
    terms = cross_terms(initial, adjoint, again_wide, adjoint_wide, again_narrow, adjoint_narrow)
    small, large = lax.psum((terms[0], terms[1]), ("wide", "narrow"))
    size_small = initial.shape[0]
    size_large = initial.shape[3]
    small = small / math.sqrt(size_small * size_large * size_large)
    large = large / math.sqrt(size_small * size_small * size_large)
    grad_small = open_small * (small - jnp.diagonal(small, axis1=1, axis2=2)[:, :, None])
    grad_large = open_large * (large - jnp.diagonal(large, axis1=1, axis2=2)[:, :, None])
    return (grad_small, grad_large)


def solution(mesh):
    line = mesh.shape["narrow"] == 4 and mesh.shape["wide"] == 8
    return jax.shard_map(
        line_device if line else on_device,
        mesh=mesh,
        in_specs=(
            P(None, "wide", "narrow", None),
            P(None, "wide", "narrow", None),
            P(),
            P(),
            P(),
            P(),
            P(),
            P(),
            P(),
            P(),
        ),
        out_specs=(P(), P()),
        check_vma=False,
    )
```

```python
import functools
import math

import jax
import jax.numpy as jnp
from jax import lax
from jax.experimental import pallas as pl
from jax.experimental.pallas import tpu as pltpu
from jax.sharding import PartitionSpec as P

highest = lax.Precision.HIGHEST
f32 = jnp.float32
VMEM_LIMIT = 40 * 1024 * 1024
bf16 = jnp.bfloat16

TO_INNER = [(0, 1), (3, 2)]
INNER_SWAP = [(1, 2), (2, 1)]
TO_OUTER = [(1, 0), (2, 3)]

PIECES = [(0, 2), (2, 4), (4, 6), (6, 7), (7, 8)]

ROWS_BY_ROWS = (((1,), (1,)), ((), ()))
DEPTH_BY_DEPTH = (((0,), (0,)), ((), ()))


def generator(rate_matrix, pattern):
    extent = rate_matrix.shape[-1]
    identity = jnp.eye(extent, dtype=jnp.float32)
    opened = pattern.astype(jnp.float32) * (1.0 - identity)
    flow_rates = rate_matrix * opened
    leaving = jnp.sum(flow_rates, axis=-1)
    return (flow_rates - leaving[..., :, None] * identity, leaving, opened)


def halves(value):
    high = value.astype(bf16)
    low = (value - high.astype(f32)).astype(bf16)
    return high, low


def run(body, grid, in_specs, out_specs, out_shape, args, done, limit=VMEM_LIMIT):
    count, extra = len(args), len(done)

    def kernel(*refs):
        body(*refs[:count], *refs[count + extra :])

    return pl.pallas_call(
        kernel,
        grid=grid,
        in_specs=list(in_specs) + [pl.BlockSpec(memory_space=pltpu.HBM)] * extra,
        out_specs=out_specs,
        out_shape=out_shape,
        compiler_params=pltpu.CompilerParams(vmem_limit_bytes=limit),
        cost_estimate=pl.CostEstimate(flops=0, bytes_accessed=0, transcendentals=0),
    )(*args, *done)


def whole(array):
    return pl.BlockSpec(array.shape, lambda i: (0,) * array.ndim)


def stacked_rows(ref, count, inner, at):
    rows = [ref[pl.ds(at + k, count, stride=inner), :] for k in (0, 1)]
    high, low = halves(jnp.concatenate(rows, axis=1))
    return jnp.concatenate([high, low], axis=0)


def left_parts(matrix):
    high, low = halves(matrix)
    return jnp.concatenate(
        [jnp.concatenate([high, high], axis=1), jnp.concatenate([low, low], axis=1)], axis=0
    )


def folded(total):
    rows, cols = total.shape[0] // 2, total.shape[1] // 2
    total = total[:rows] + total[rows:]
    return total[:, :cols] + total[:, cols:]


def product(matrix, in_ref, out_ref, count, inner, add):
    width = in_ref.shape[1]
    for at in range(0, inner, 2):
        out = jnp.dot(matrix, stacked_rows(in_ref, count, inner, at), preferred_element_type=f32)
        out = out[:count] + out[count:]
        for k in (0, 1):
            place = pl.ds(at + k, count, stride=inner)
            piece = out[:, k * width : (k + 1) * width]
            out_ref[place, :] = out_ref[place, :] + piece if add else piece


def base_body(x_ref, t_ref, first_ref, last_ref, o_ref):
    count, _, inner, width = x_ref.shape
    x2, t2, o2 = (ref.reshape(count * inner, width) for ref in (x_ref, t_ref, o_ref))
    high, low = halves(last_ref[...])
    last = jnp.concatenate([jnp.concatenate([high, low], axis=1)] * 2, axis=0)
    for r in range(0, count * inner, 256):
        x = x2[r : r + 256]
        high, low = halves(x)
        out = jnp.dot(jnp.concatenate([high, low], axis=1), last, preferred_element_type=f32)
        o2[r : r + 256] = x - t2[r : r + 256] + (out[:, :width] + out[:, width:])
    product(left_parts(first_ref[...]), x2, o2, count, inner, True)


def base_terms(x, t, first, last, *done):
    block = pl.BlockSpec((x.shape[0], 1) + x.shape[2:], lambda i: (0, i, 0, 0))
    return run(
        base_body,
        (x.shape[1],),
        [block, block, whole(first), whole(last)],
        block,
        jax.ShapeDtypeStruct(x.shape, f32),
        (x, t, first, last,),
        done,
    )


def one_body(x_ref, k_ref, o_ref):
    blocks, _, rows, inner, width = x_ref.shape
    count = blocks * rows
    x2, o2 = x_ref.reshape(count * inner, width), o_ref.reshape(count * inner, width)
    product(left_parts(k_ref[0]), x2, o2, count, inner, False)


def one_terms(x, matrices, skip, states, *done):
    block = lambda skip: pl.BlockSpec((x.shape[0], 1) + x.shape[2:], lambda i: (0, i + skip, 0, 0, 0))
    return run(
        one_body,
        (states,),
        [block(skip), pl.BlockSpec((1,) + matrices.shape[1:], lambda i: (i + skip, 0, 0))],
        block(0),
        jax.ShapeDtypeStruct((x.shape[0], states) + x.shape[2:], f32),
        (x, matrices,),
        done,
    )


def one_cross_body(x_ref, a_ref, o_ref):
    blocks, _, rows, inner, width = x_ref.shape
    count = blocks * rows
    x2, a2 = x_ref.reshape(count * inner, width), a_ref.reshape(count * inner, width)
    total = None
    for at in range(0, inner, 2):
        term = lax.dot_general(
            stacked_rows(x2, count, inner, at),
            stacked_rows(a2, count, inner, at),
            ROWS_BY_ROWS,
            preferred_element_type=f32,
        )
        total = term if total is None else total + term
    o_ref[0] = folded(total)


def one_cross(x, a, skip, *done):
    count = x.shape[0] * x.shape[2]
    shape = (x.shape[0], 1) + x.shape[2:]
    out = run(
        one_cross_body,
        (a.shape[1],),
        [
            pl.BlockSpec(shape, lambda i: (0, i + skip, 0, 0, 0)),
            pl.BlockSpec(shape, lambda i: (0, i, 0, 0, 0)),
        ],
        pl.BlockSpec((1, count, count), lambda i: (i, 0, 0)),
        jax.ShapeDtypeStruct((a.shape[1], count, count), f32),
        (x, a,),
        done,
    )
    return out


def local_body(pieces, x_ref, *refs):
    a_refs, o_ref, o3_ref = refs[: len(pieces)], refs[-2], refs[-1]
    wide, deep, _, inner, width = x_ref.shape
    x2 = x_ref.reshape(wide * deep * inner, width)
    flat = [a.reshape(a.shape[0] * a.shape[1] * inner, width) for a in a_refs]
    total = None
    for at in range(0, inner, 2):
        parts = []
        for k in (0, 1):
            rows = [
                a[pl.ds(at + k, wide * (hi - lo), stride=inner), :] for a, (lo, hi) in zip(flat, pieces)
            ]
            parts.append(jnp.concatenate(rows, axis=0))
        high, low = halves(jnp.concatenate(parts, axis=1))
        term = lax.dot_general(
            stacked_rows(x2, wide * deep, inner, at),
            jnp.concatenate([high, low], axis=0),
            ROWS_BY_ROWS,
            preferred_element_type=f32,
        )
        total = term if total is None else total + term
    o_ref[0] = folded(total)
    total = None
    for a_ref, (lo, hi) in zip(a_refs, pieces):
        for s in range(lo, hi):
            sides = []
            for ref, at in ((x_ref, s), (a_ref, s - lo)):
                rows = jnp.concatenate([ref[w, at, 0] for w in range(wide)], axis=0)
                sides.append(jnp.concatenate(halves(rows), axis=1))
            term = lax.dot_general(sides[0], sides[1], DEPTH_BY_DEPTH, preferred_element_type=f32)
            total = term if total is None else total + term
    o3_ref[0] = folded(total)


def local_cross(x, adjoints, *done):
    wide, deep, rows, inner, width = x.shape
    block = lambda a: pl.BlockSpec((wide, a.shape[1], 1, inner, width), lambda i: (0, 0, i, 0, 0))
    count = wide * deep
    zero, three = run(
        functools.partial(local_body, PIECES),
        (rows,),
        [block(x)] + [block(a) for a in adjoints],
        [
            pl.BlockSpec((1, count, count), lambda i: (i, 0, 0)),
            pl.BlockSpec((1, width, width), lambda i: (i, 0, 0)),
        ],
        [
            jax.ShapeDtypeStruct((rows, count, count), f32),
            jax.ShapeDtypeStruct((rows, width, width), f32),
        ],
        (x, *adjoints,),
        done,
        56 * 1024 * 1024,
    )
    zero = jnp.sum(zero, axis=0)
    columns, at = [], 0
    for lo, hi in PIECES:
        size = wide * (hi - lo)
        columns.append(zero[:, at : at + size].reshape(count, wide, hi - lo))
        at += size
    zero = jnp.concatenate(columns, axis=2).reshape(count, count)
    return zero, jnp.sum(three, axis=0)


def block_pair(refs, n):
    sides = [jnp.concatenate([ref[k] for ref in refs], axis=0) for k in (n, n + 1)]
    high, low = halves(jnp.concatenate(sides, axis=1))
    return jnp.concatenate([high, low], axis=0)


def pair_terms_body(w_ref, m_ref, x_ref, p_ref, q_ref, f_ref, own_ref, other_ref):
    cells, part, width = x_ref.shape
    weights = left_parts(m_ref[...])
    gate = jnp.concatenate([w_ref[...], w_ref[...]], axis=1)
    for n in range(0, cells, 2):
        both = block_pair((x_ref, p_ref, q_ref, f_ref), n)
        out = jnp.dot(weights, both, preferred_element_type=f32)
        rows = out.shape[0] // 2
        out = out[:rows] + out[rows:]
        out = out[: rows // 2] + gate * out[rows // 2 :]
        for k in (0, 1):
            own_ref[n + k] = out[:part, k * width : (k + 1) * width]
            other_ref[n + k] = out[part:, k * width : (k + 1) * width]


def pair_cross_body(x_ref, p_ref, q_ref, f_ref, own_ref, base_ref, terms_ref, c_ref):
    total = None
    for n in range(0, x_ref.shape[0], 2):
        sides = [
            jnp.concatenate([own_ref[k], base_ref[k] + terms_ref[k]], axis=0) for k in (n, n + 1)
        ]
        high, low = halves(jnp.concatenate(sides, axis=1))
        term = lax.dot_general(
            block_pair((x_ref, p_ref, q_ref, f_ref), n),
            jnp.concatenate([high, low], axis=0),
            ROWS_BY_ROWS,
            preferred_element_type=f32,
        )
        total = term if total is None else total + term
    c_ref[0] = folded(total)


def pair_terms(gate, weights, blocks, *done):
    count, part, width = blocks[0].shape
    cells = 16
    block = pl.BlockSpec((cells, part, width), lambda i: (i, 0, 0))
    return run(
        pair_terms_body,
        (count // cells,),
        [whole(gate), whole(weights)] + [block] * 4,
        [block, block],
        [jax.ShapeDtypeStruct(blocks[0].shape, f32)] * 2,
        (gate, weights, *blocks,),
        done,
    )


def pair_cross(blocks, *done):
    count, part, width = blocks[0].shape
    cells = 16
    block = pl.BlockSpec((cells, part, width), lambda i: (i, 0, 0))
    shape = (count // cells, 4 * part, 2 * part)
    return run(
        pair_cross_body,
        (count // cells,),
        [block] * 7,
        pl.BlockSpec((1,) + shape[1:], lambda i: (i, 0, 0)),
        jax.ShapeDtypeStruct(shape, f32),
        (*blocks,),
        done,
    )


def last_body(scale_small, scale_large, a_ref, b_ref, small_ref, large_ref, s_ref, l_ref):
    total = a_ref[...] + b_ref[...]

    def gradient(cross, opened):
        same = lax.broadcasted_iota(jnp.int32, cross.shape, 0) == lax.broadcasted_iota(jnp.int32, cross.shape, 1)
        diagonal = jnp.sum(jnp.where(same, cross, 0.0), axis=1, keepdims=True)
        return opened * (cross - diagonal)

    small, large = s_ref.shape[1], l_ref.shape[1]
    for k in (0, 1):
        cross = total[:small, k * small : (k + 1) * small] / scale_small
        s_ref[k] = gradient(cross, small_ref[k])
        cross = total[small + k * large : small + (k + 1) * large] / scale_large
        l_ref[k] = gradient(cross, large_ref[k])


def copy_body(x_ref, o_ref):
    o_ref[...] = x_ref[...]


def sum_body(*refs):
    total = refs[0][...]
    for ref in refs[1:-1]:
        total = total + ref[...]
    refs[-1][...] = total


def piece_of(lo, hi, skip, shape):
    size = hi - lo
    return pl.BlockSpec((1, size) + shape[2:], lambda i: (i, (lo - skip) // size, 0, 0, 0))


def cut_piece(x, lo, hi, *done):
    out = jax.ShapeDtypeStruct((x.shape[0], hi - lo) + x.shape[2:], f32)
    return run(
        copy_body, (x.shape[0],), [piece_of(lo, hi, 0, x.shape)], piece_of(lo, hi, lo, x.shape), out, (x,), done
    )


def add_piece(x, y, skip, lo, hi, *done):
    out = jax.ShapeDtypeStruct((x.shape[0], hi - lo) + x.shape[2:], f32)
    return run(
        sum_body,
        (x.shape[0],),
        [piece_of(lo, hi, 0, x.shape), piece_of(lo, hi, skip, x.shape)],
        piece_of(lo, hi, lo, x.shape),
        out,
        (x, y),
        done,
    )


def add_all(arrays, *done):
    shape = arrays[0].shape
    block = pl.BlockSpec((shape[0] // 4,) + shape[1:], lambda i: (i, 0, 0))
    out = jax.ShapeDtypeStruct(shape, f32)
    return run(sum_body, (4,), [block] * len(arrays), block, out, tuple(arrays), done)


def line_device(
    initial, target, rates_small, rates_large, pattern_small, pattern_large,
    spare_small, spare_large, trigger_first, trigger_last,
):
    gen_small, exit_small, open_small = generator(rates_small, pattern_small)
    gen_large, exit_large, open_large = generator(rates_large, pattern_large)
    rim_one = jnp.sum(spare_small, axis=1)
    rim_two = jnp.sum(spare_large, axis=1)
    weight_first = trigger_first.astype(f32)
    weight_last = trigger_last.astype(f32)
    bound = jnp.sum(jnp.max(exit_small, axis=1)) + jnp.sum(jnp.max(exit_large, axis=1))
    bound = bound + jnp.max(weight_first) * jnp.max(rim_one) + jnp.max(weight_last) * jnp.max(rim_two)
    step_size = 1.0 / bound

    size_small, size_large = initial.shape[0], initial.shape[3]
    wide = lax.axis_size("wide")
    wide_pos = lax.axis_index("wide")
    place = lax.axis_index("narrow")
    deep = size_small // wide
    rows, part = initial.shape[1], initial.shape[2]

    spare_one = spare_small - jnp.diag(rim_one)
    mine = lax.dynamic_slice_in_dim(weight_first, wide_pos * deep, deep)
    mode_one = step_size * (gen_small[1][None] + mine[:, None, None] * spare_one[None])
    mode_one = mode_one.transpose(0, 2, 1)

    inner = (place == 1) | (place == 2)
    partner = jnp.where(place < 2, 1 - place, 5 - place)
    spare_two = spare_large - jnp.diag(rim_two)
    factor = jnp.where(inner, step_size, 0.0)
    places = jnp.concatenate(
        [jnp.arange(part) + block * part for block in (place, partner, 3 - place, 3 - partner)]
    )
    spread = (places[:, None] == jnp.arange(size_large)[None]).astype(f32)
    picked = functools.partial(jnp.einsum, "xr,rc,yc->xy", precision=highest)
    weights = factor * jnp.concatenate(
        [picked(spread, m, spread[: 2 * part]) for m in (gen_large[0], spare_two)], axis=1
    ).T
    gate = weight_last[None, :]

    xv = initial.reshape(wide, deep, rows, part, size_large)
    half = deep // 2

    def shift(value, pairs):
        return lax.ppermute(value, "narrow", pairs)

    def exchange(value):
        return lax.all_to_all(value, "wide", 0, 0, tiled=True)

    count = len(PIECES)
    xs, ps, qs, fs = ([None] * count for _ in range(4))
    bases, others, own, other, far = ([None] * count for _ in range(5))
    adjoints, wide_a, ones, twos = ([None] * count for _ in range(4))

    def flat(value):
        return value.reshape(-1, part, size_large)

    def send_piece(k, *done):
        xs[k] = flat(cut_piece(xv, *PIECES[k], *done))
        ps[k] = shift(xs[k], TO_INNER)
        qs[k] = shift(xs[k], INNER_SWAP)
        fs[k] = shift(ps[k], INNER_SWAP)

    def base_step(k, *done):
        lo, hi = PIECES[k]
        bases[k] = flat(add_piece(base.reshape(xv.shape), back[lo // half], lo // half * half, lo, hi, *done))
        others[k] = shift(bases[k], TO_INNER)

    def terms_step(k, *done):
        own[k], other[k] = pair_terms(gate, weights, (xs[k], ps[k], qs[k], fs[k]), *done)
        far[k] = shift(other[k], TO_OUTER)

    def finish(k, *done):
        lo, hi = PIECES[k]
        total = add_all((own[k], far[k], bases[k]), *done)
        adjoints[k] = total.reshape(wide, hi - lo, rows, part, size_large)
        wide_a[k] = exchange(adjoints[k])

    def one_step(k, *done):
        ones[k] = one_cross(wide_x, wide_a[k], PIECES[k][0], *done)

    def two_step(k, *done):
        twos[k] = pair_cross((xs[k], ps[k], qs[k], fs[k], flat(adjoints[k]), others[k], other[k]), *done)

    wide_x = exchange(xv)
    send_piece(0)
    send_piece(1)
    for k in (2, 3, 4):
        send_piece(k, xs[1])
    base = base_terms(initial, target, step_size * gen_small[0].T, step_size * gen_large[1], xs[4])
    one_first = one_terms(wide_x, mode_one, 0, half, base, ps[0], qs[0], ps[1], qs[1])
    one_second = one_terms(wide_x, mode_one, half, deep - half, one_first)
    back = [exchange(one_first), exchange(one_second)]
    terms_step(0, one_second)
    base_step(0, own[0])
    base_step(1, bases[0])
    terms_step(1, bases[1], ps[2], ps[3], ps[4])
    base_step(2, own[1])
    base_step(3, bases[2])
    base_step(4, bases[3])
    finish(0, bases[4])
    terms_step(2, adjoints[0])
    finish(1, own[2])
    two_step(0, adjoints[1])
    two_step(1, twos[0])
    terms_step(3, twos[1])
    finish(2, own[3])
    one_step(0, adjoints[2])
    one_step(1, ones[0])
    two_step(2, ones[1])
    terms_step(4, twos[2], others[3], others[4])
    finish(3, own[4])
    one_step(2, adjoints[3])
    two_step(3, ones[2])
    finish(4, twos[3])
    cross_zero, cross_three = local_cross(xv, adjoints)
    two_step(4, cross_three)
    one_step(3, twos[4])
    one_step(4, ones[3])
    cross_one = jnp.sum(jnp.concatenate(ones, axis=0), axis=0)
    found = jnp.where(inner, jnp.sum(jnp.concatenate(twos, axis=0), axis=0), 0.0)
    cross_two = jnp.einsum("xr,xy,yc->rc", spread, found, spread[: 2 * part], precision=highest)

    packed = jnp.concatenate(
        [jnp.concatenate([cross_zero, cross_one], axis=1), cross_two, cross_three], axis=0
    )
    def partner(value, axis, step):
        return lax.ppermute(value, axis, [(i, i ^ step) for i in range(lax.axis_size(axis))])

    for axis, step in (("wide", 1), ("wide", 2), ("wide", 4), ("narrow", 1)):
        packed = packed + partner(packed, axis, step)
    arrays = (packed, partner(packed, "narrow", 2), open_small, open_large)
    grad_small, grad_large = run(
        functools.partial(
            last_body,
            math.sqrt(size_small * size_large * size_large),
            math.sqrt(size_small * size_small * size_large),
        ),
        (1,),
        [whole(array) for array in arrays],
        [whole(open_small), whole(open_large)],
        [jax.ShapeDtypeStruct(open_small.shape, f32), jax.ShapeDtypeStruct(open_large.shape, f32)],
        arrays,
        (),
    )
    return (grad_small, grad_large)


def enter_first(tensor):
    return lax.all_to_all(tensor, "wide", split_axis=0, concat_axis=1, tiled=True)


def leave_first(tensor):
    return lax.all_to_all(tensor, "wide", split_axis=1, concat_axis=0, tiled=True)


def enter_second(tensor):
    return lax.all_to_all(tensor, "narrow", split_axis=0, concat_axis=2, tiled=True)


def leave_second(tensor):
    return lax.all_to_all(tensor, "narrow", split_axis=2, concat_axis=0, tiled=True)


def rearranged(tensor):
    return (enter_first(tensor), enter_second(tensor))


def local_part(tensor, mode_zero, mode_three):
    local_terms = jnp.einsum("abcd,ae->ebcd", tensor, mode_zero, precision=highest)
    return local_terms + jnp.einsum("abcd,de->abce", tensor, mode_three, precision=highest)


def operate(tensor, matrices, weights):
    mode_zero, mode_one, mode_two, mode_three, spare_one, spare_two, rim_one, rim_two = matrices
    weight_part, weight_last, weight_tail = weights
    local_terms = local_part(tensor, mode_zero, mode_three)
    tensor_wide = enter_first(tensor)
    tensor_narrow = enter_second(tensor)
    lifted = tensor_wide * weight_part[:, None, None, None]
    wide_terms = jnp.einsum("abcd,be->aecd", tensor_wide, mode_one, precision=highest)
    wide_terms = (
        wide_terms
        + jnp.einsum("abcd,be->aecd", lifted, spare_one, precision=highest)
        - lifted * rim_one[None, :, None, None]
    )
    lowered = tensor_narrow * weight_last[None, None, None, :]
    narrow_terms = jnp.einsum("abcd,ce->abed", tensor_narrow, mode_two, precision=highest)
    narrow_terms = (
        narrow_terms
        + jnp.einsum("abcd,ce->abed", lowered, spare_two, precision=highest)
        - lowered * rim_two[None, None, :, None]
    )
    return (
        local_terms + leave_first(wide_terms) + leave_second(narrow_terms),
        tensor_wide,
        tensor_narrow,
    )


def cross_terms(state_prev, adjoint_now, state_wide, adjoint_wide, state_narrow, adjoint_narrow):
    cross_zero = jnp.einsum("abcd,ebcd->ae", state_prev, adjoint_now, precision=highest)
    cross_three = jnp.einsum("abcd,abce->de", state_prev, adjoint_now, precision=highest)
    cross_one = jnp.einsum("abcd,aecd->be", state_wide, adjoint_wide, precision=highest)
    cross_two = jnp.einsum("abcd,abed->ce", state_narrow, adjoint_narrow, precision=highest)
    return (jnp.stack([cross_zero, cross_one]), jnp.stack([cross_two, cross_three]))


def on_device(
    initial,
    target,
    rates_small,
    rates_large,
    pattern_small,
    pattern_large,
    spare_small,
    spare_large,
    trigger_first,
    trigger_last,
):
    gen_small, exit_small, open_small = generator(rates_small, pattern_small)
    gen_large, exit_large, open_large = generator(rates_large, pattern_large)
    rim_one = jnp.sum(spare_small, axis=1)
    rim_two = jnp.sum(spare_large, axis=1)
    weight_first = trigger_first.astype(jnp.float32)
    weight_last = trigger_last.astype(jnp.float32)
    bound = jnp.sum(jnp.max(exit_small, axis=1)) + jnp.sum(jnp.max(exit_large, axis=1))
    bound = (
        bound + jnp.max(weight_first) * jnp.max(rim_one) + jnp.max(weight_last) * jnp.max(rim_two)
    )
    step_size = 1.0 / bound
    wide_pos = lax.axis_index("wide")
    rows_wide = initial.shape[0] // lax.axis_size("wide")
    weight_part = lax.dynamic_slice_in_dim(weight_first, wide_pos * rows_wide, rows_wide)
    narrow_pos = lax.axis_index("narrow")
    rows_narrow = initial.shape[3] // lax.axis_size("narrow")
    weight_tail = lax.dynamic_slice_in_dim(weight_last, narrow_pos * rows_narrow, rows_narrow)
    weights = (weight_part, weight_last, weight_tail)
    onward = (
        gen_small[0],
        gen_small[1],
        gen_large[0],
        gen_large[1],
        spare_small,
        spare_large,
        rim_one,
        rim_two,
    )
    new_terms, start_wide, start_narrow = operate(initial, onward, weights)
    state = initial + step_size * new_terms
    adjoint = state - target
    adjoint_wide, adjoint_narrow = rearranged(adjoint)
    again_wide, again_narrow = rearranged(initial)
    terms = cross_terms(initial, adjoint, again_wide, adjoint_wide, again_narrow, adjoint_narrow)
    small, large = lax.psum((terms[0], terms[1]), ("wide", "narrow"))
    size_small = initial.shape[0]
    size_large = initial.shape[3]
    small = small / math.sqrt(size_small * size_large * size_large)
    large = large / math.sqrt(size_small * size_small * size_large)
    grad_small = open_small * (small - jnp.diagonal(small, axis1=1, axis2=2)[:, :, None])
    grad_large = open_large * (large - jnp.diagonal(large, axis1=1, axis2=2)[:, :, None])
    return (grad_small, grad_large)


def solution(mesh):
    line = mesh.shape["narrow"] == 4 and mesh.shape["wide"] == 8
    return jax.shard_map(
        line_device if line else on_device,
        mesh=mesh,
        in_specs=(
            P(None, "wide", "narrow", None),
            P(None, "wide", "narrow", None),
            P(),
            P(),
            P(),
            P(),
            P(),
            P(),
            P(),
            P(),
        ),
        out_specs=(P(), P()),
        check_vma=False,
    )
```
